512 devices in a mesh: expert: 8 (over z_lo), etp: 32 (over x, y, z_hi), dp: 2 (over core).
Axes of the slice: x: 4, y: 4, z: 16 (z_hi: 2, z_lo: 8; z = z_hi * 8 + z_lo), core: 2. Of those that a mesh axis runs over, the one named last changes fastest.
Arguments:
- out_grad: bfloat16 [4096, 3072], P(('expert', 'etp', 'dp')), may hold values from -0.59765625 to 0.59765625
- routes: int32 [4096, 2], P(('expert', 'etp', 'dp')), may hold values from 0 to 7, all different within a row; in each aligned block of 8 rows (0 to 7, 8 to 15, ...) at most 4 rows name the same one
- route_weight: bfloat16 [4096, 2], P(('expert', 'etp', 'dp')), may hold values from 0.099609375 to 1
- saved_act: bfloat16 [2, 2, 8, 1024, 8192], P(None, 'dp', 'expert', None, 'etp'), may hold values from -6 to 6
- w_down: bfloat16 [8, 8192, 3072], P('expert', 'etp'), may hold values from -0.109375 to 0.109375
Outputs:
- d_act: bfloat16 [2, 2, 8, 1024, 8192], P(None, 'dp', 'expert', None, 'etp')
- d_weight: bfloat16 [8, 8192, 3072], P('expert', 'etp', 'dp')
- d_route: float32 [4096, 2], P(('expert', 'etp', 'dp'))
The draws below stay inside these ranges and needn't reach their ends.
Inputs may be any that keep to these rules, and one draw needn't show every extreme that they name: `routes`: A token's two experts differ. Among the 8 tokens of one device (an aligned block of rows) no expert is named more than 4 times, and in every draw some device names some expert exactly 4 times.
All inputs are finite; a program needn't handle non-finite values.
Results may differ from the reference program's by a relative error of at most 0.0049.
Values may be sent and summed in bfloat16 or wider, within the bound.
A program may use at most 64 MiB of HBM per device.

```python
import math
import jax
import jax.numpy as jnp
import numpy as np

D = 3072
FF = 8192
TOPK = 2
TOK_DEV = 8
EXPERTS = 8
CAP = 4
TOKENS = 4096
ROWS = 1024
N_EXPERT = 8
N_ETP = 32
N_DP = 2


def levels(rng, extent, shards, least, largest):
    gain = 1.0
    for dim, blocks in shards:
        heights = jax.random.uniform(jax.random.fold_in(jax.random.fold_in(rng, 6), dim), (blocks,), jnp.float32, least / len(shards), largest / len(shards))
        gain = gain * jnp.repeat(jnp.exp(heights), extent[dim] // blocks).reshape((-1,) + (1,) * (len(extent) - 1 - dim))
    return gain


def assign_block(rng, own, number, rows, amount, top, most, lean):
    order = jax.random.permutation(rng, amount)
    packed, ordinary = shares(amount, rows * top, most, lean, True), shares(amount, rows * top, most, lean, False)
    places = jnp.arange(amount)

    def named(tallies, rotation):
        used = int((tallies > 0).sum())
        fixed = max(1, used // 4)
        shifted = fixed + (places - fixed + rotation * (used - fixed)) % max(1, amount - fixed)
        return jnp.zeros((amount,), jnp.int32).at[order[jnp.where(places < fixed, places, shifted)]].set(jnp.asarray(tallies, jnp.int32))

    tallies = jnp.where(number % 4 == 0, named(packed, number // 4), named(ordinary, number - number // 4 - 1))
    mixed = jax.random.permutation(jax.random.fold_in(own, 3), amount)
    giver, receiver = mixed[0:amount // 2 * 2:2], mixed[1:amount // 2 * 2:2]
    margin = jnp.minimum(tallies[giver] - 1, most - tallies[receiver]) // 2
    margin = jnp.where((giver == order[0]) | (receiver == order[0]) | (tallies[receiver] == 0), 0, jnp.maximum(margin, 0))
    shifted = jax.random.randint(jax.random.fold_in(own, 4), (amount // 2,), 0, 1 << 20) % (margin + 1)
    tallies = tallies.at[giver].add(-shifted).at[receiver].add(shifted)
    members = jnp.searchsorted(jnp.cumsum(tallies), jnp.arange(rows * top), side="right").astype(jnp.int32)
    table = members.reshape(top, rows).T
    table = table[jax.random.permutation(jax.random.fold_in(own, 1), rows)]
    rotation = jax.random.randint(jax.random.fold_in(own, 2), (rows, 1), 0, top)
    return jnp.take_along_axis(table, (jnp.arange(top)[None, :] + rotation) % top, axis=1)


def shares(count, total, most, slope, full):
    weights = [(1 << 20) // math.isqrt(grade ** slope) + 1 for grade in range(1, count + 1)]
    largest = most if full else min(most, max(-(-total // count), total * weights[0] // sum(weights)))
    least = 1 if total - largest >= count - 1 else 0
    counts, spare = [largest] + [least] * (count - 1), total - largest - least * (count - 1)
    while spare > 0:
        movable = [i for i in range(1, count) if counts[i] < largest] or [i for i in range(1, count) if counts[i] < most]
        pool, left = sum([weights[i] for i in movable]), spare
        for i in movable:
            extra = min(most - counts[i], max(1, left * weights[i] // pool), spare)
            counts[i] = counts[i] + extra
            spare = spare - extra
    return np.array(counts)


def centred(own_key, extent, width, reach, shards=(), held_as=jnp.bfloat16):
    values = jax.random.normal(own_key, extent, jnp.float32) * width
    if len(shards) > 0:
        values = levels(own_key, extent, shards, -0.22, 0.18) * values
    return jnp.clip(values, min=-reach, max=reach).astype(held_as)


def setup_inputs(seed: int = 0) -> dict:
    arg_keys = jax.random.split(jax.random.key(seed), 6)
    out_grad = centred(arg_keys[0], (TOKENS, D), 0.1, 0.59765625, ((0, 512),))
    routes_keys = jax.random.split(jax.random.fold_in(arg_keys[1], 1), TOKENS // TOK_DEV)
    routes_turns = jax.random.permutation(jax.random.fold_in(arg_keys[1], 3), TOKENS // TOK_DEV)
    routes = jax.vmap(lambda own, number: assign_block(jax.random.fold_in(arg_keys[1], 2), own, number, TOK_DEV, EXPERTS, TOPK, CAP, 2))(routes_keys, routes_turns).reshape((TOKENS, TOPK))
    route_weight = jnp.clip(0.099609375 + 0.9003906 * jax.random.uniform(arg_keys[2], (TOKENS, TOPK), jnp.float32) ** levels(arg_keys[2], (TOKENS, TOPK), ((0, 512),), -0.2, 0.2), 0.099609375, 1.0).astype(jnp.bfloat16)
    saved_act = centred(arg_keys[3], (2, N_DP, EXPERTS, ROWS, FF), 1.0, 6.0, ((1, 2), (2, 8), (4, 32)))
    w_down = centred(arg_keys[4], (EXPERTS, FF, D), D ** -0.5, 0.109375, ((0, 8), (1, 32)))
    return {"out_grad": out_grad, "routes": routes, "route_weight": route_weight, "saved_act": saved_act, "w_down": w_down}


def slot_layout(routes):
    device_count = N_EXPERT * N_ETP * N_DP
    flat_routes = routes.reshape(device_count, TOK_DEV * TOPK).astype(jnp.int32)
    one_hot = (flat_routes[:, :, None] == jnp.arange(EXPERTS, dtype=jnp.int32)[None, None, :]).astype(jnp.int32)
    slot_rank = jnp.sum((jnp.cumsum(one_hot, axis=1) - one_hot) * one_hot, axis=2)
    device_ids = jnp.arange(device_count, dtype=jnp.int32)
    source_expert = device_ids // (N_ETP * N_DP)
    source_etp = (device_ids // N_DP) % N_ETP
    replica_ids = device_ids % N_DP
    row_index = ((source_etp[:, None] * EXPERTS + source_expert[:, None]) * CAP + slot_rank).astype(jnp.int32)
    replica_index = jnp.broadcast_to(replica_ids[:, None], row_index.shape).astype(jnp.int32)
    return flat_routes, row_index, replica_index


def reference(out_grad, routes, route_weight, saved_act, w_down):
    device_count = N_EXPERT * N_ETP * N_DP
    flat_routes, row_index, replica_index = slot_layout(routes)
    repeated = jnp.repeat(out_grad.reshape(device_count, TOK_DEV, D), TOPK, axis=1)
    weights_flat = route_weight.reshape(device_count, TOK_DEV * TOPK).astype(jnp.float32)
    expert_rows = jnp.zeros((N_DP, EXPERTS, ROWS, D), out_grad.dtype).at[replica_index, flat_routes, row_index].set(repeated)
    row_weights = jnp.zeros((N_DP, EXPERTS, ROWS), jnp.float32).at[replica_index, flat_routes, row_index].set(weights_flat)
    act_replicas = []
    part_replicas = []
    grad_experts = []
    for expert in range(EXPERTS):
        grad_sum = jnp.zeros((FF, D), jnp.float32)
        for replica in range(N_DP):
            gate_pre = saved_act[0, replica, expert].astype(jnp.float32)
            up_pre = saved_act[1, replica, expert].astype(jnp.float32)
            gate_sig = jax.nn.sigmoid(gate_pre)
            hidden = gate_pre * gate_sig * up_pre
            row_weight = row_weights[replica, expert]
            weighted = (row_weight[:, None] * hidden).astype(jnp.bfloat16)
            rows_here = expert_rows[replica, expert]
            grad_sum = grad_sum + jnp.dot(weighted.T, rows_here, preferred_element_type=jnp.float32)
            d_out = jnp.dot(rows_here, w_down[expert].T, preferred_element_type=jnp.float32)
            d_hidden = row_weight[:, None] * d_out
            d_gate = (d_hidden * up_pre * gate_sig * (1.0 + gate_pre * (1.0 - gate_sig))).astype(jnp.bfloat16)
            d_up = (d_hidden * gate_pre * gate_sig).astype(jnp.bfloat16)
            act_replicas.append(jnp.stack([d_gate, d_up]))
            part_replicas.append(jnp.sum(hidden * d_out, axis=1))
        grad_experts.append(grad_sum.astype(jnp.bfloat16))
    act_table = jnp.stack(act_replicas).reshape(EXPERTS, N_DP, 2, ROWS, FF)
    d_act = jnp.transpose(act_table, (2, 1, 0, 3, 4))
    partial_table = jnp.transpose(jnp.stack(part_replicas).reshape(EXPERTS, N_DP, ROWS), (1, 0, 2))
    d_route = partial_table[replica_index, flat_routes, row_index].reshape(TOKENS, TOPK)
    d_weight = jnp.stack(grad_experts)
    return d_act, d_weight, d_route
```

```python
import jax
import jax.numpy as jnp
from jax import lax
from jax.experimental import pallas as pl
from jax.experimental.pallas import tpu as pltpu
from jax.sharding import PartitionSpec as P

MESH = pl.DeviceIdType.MESH
F32 = jnp.float32
BF16 = jnp.bfloat16
D = 3072
HALF = D // 2
FOLD = D // 4
ORDER = (0, 1, 3, 2)


def iota(shape, axis):
    return lax.broadcasted_iota(jnp.int32, shape, axis)


def kernel(
    tok_ref, route_ref, weight_ref, act_hbm, w_hbm,
    dact_hbm, dw_hbm, droute_ref,
    act, w, wt, outgoing, zbuf, rows, hid, cgate, cup, hidt, dact, grad, grad_in, dw,
    psum, psum_in, colsum, colsum_in,
    local_sem, zsend, zrecv, gsend, grecv, psend, precv, csend, crecv, xsend, xrecv,
):
    e = lax.axis_index("expert")
    t = lax.axis_index("etp")
    p = lax.axis_index("dp")
    x, y, zh = t // 8, (t // 2) % 4, t % 2
    z = zh * 8 + e
    quad = z // 4
    col = x * 4 + y

    def at(xx, yy, zz):
        return (zz % 8, xx * 8 + yy * 2 + zz // 8, p)

    def at_col(cc):
        return at(cc // 4, cc % 4, z)

    sibling = (e, t, 1 - p)
    xr, xl, yr, yl = (x + 1) % 4, (x + 3) % 4, (y + 1) % 4, (y + 3) % 4

    barrier = pltpu.get_barrier_semaphore()
    for k in range(1, 16):
        pl.semaphore_signal(barrier, inc=1, device_id=at(x, y, (z + k) % 16), device_id_type=MESH)
        pl.semaphore_signal(barrier, inc=1, device_id=at_col((col + k) % 16), device_id_type=MESH)
    pl.semaphore_signal(barrier, inc=1, device_id=sibling, device_id_type=MESH)

    load_act = pltpu.make_async_copy(act_hbm, act, local_sem.at[0])
    load_w = pltpu.make_async_copy(w_hbm, w, local_sem.at[1])
    load_act.start()
    load_w.start()

    spread = (iota((8, 128), 1) % 8 == iota((8, 128), 0)).astype(BF16)
    routes = jnp.dot(route_ref[...].astype(F32).astype(BF16), spread, preferred_element_type=F32)
    gates = jnp.dot(weight_ref[...], spread, preferred_element_type=F32)
    row, lane = iota((128, 128), 0), iota((128, 128), 1)
    row_e = (row // 16).astype(F32)
    first, second = routes[0:1] == row_e, routes[1:2] == row_e
    named = jnp.logical_or(first, second)
    earlier = jnp.logical_and(row // 8 == lane // 8, row < lane).astype(BF16)
    rank = jnp.dot(named.astype(F32).astype(BF16), earlier, preferred_element_type=F32)
    hit = jnp.logical_and(named, rank == (row % 4).astype(F32))
    hit = jnp.logical_and(hit, (row // 4) % 4 == lane // 8)
    pick = jnp.where(hit, jnp.where(first, gates[0:1], gates[1:2]), 0.0).astype(BF16)
    token = tok_ref[...].astype(F32)
    folded = jnp.concatenate([token[:, i * FOLD : (i + 1) * FOLD] for i in range(4)], axis=0)
    slots = jnp.dot(pick[:, 0:32], folded.astype(BF16), preferred_element_type=F32)
    outgoing[...] = slots.astype(BF16).reshape(8, 16, FOLD)

    pl.semaphore_wait(barrier, 31)

    sends = []
    for qrel in ORDER:
        for k in range(4):
            if qrel == 0 and k == 0:
                continue
            zz = ((quad + qrel) % 4) * 4 + (z + k) % 4
            copy = pltpu.make_async_remote_copy(
                src_ref=outgoing.at[zz % 8],
                dst_ref=zbuf.at[z],
                send_sem=zsend.at[len(sends)],
                recv_sem=zrecv.at[quad],
                device_id=at(x, y, zz),
                device_id_type=MESH,
            )
            copy.start()
            sends.append(copy)
    zbuf[z] = outgoing[e]

    mrow, mcol = iota((64, 64), 0), iota((64, 64), 1)
    unfold = jnp.logical_and(mrow // 16 == (mcol // 4) % 4, (mrow // 4) % 4 == mcol // 16)
    unfold = jnp.logical_and(unfold, mrow % 4 == mcol % 4).astype(F32).astype(BF16)

    def assemble(j):
        q = (quad + ORDER[j]) % 4
        count = 3 if j == 0 else 4
        landed = zbuf.at[pl.ds(0, count)]
        pltpu.make_async_copy(landed, landed, zrecv.at[q]).wait()
        block = zbuf[pl.ds(q * 4, 4)].reshape(64, FOLD)
        flat = jnp.dot(unfold, block, preferred_element_type=F32).astype(BF16)
        for i in range(4):
            rows[j, x, y, :, i * FOLD : (i + 1) * FOLD] = flat[i * 16 : (i + 1) * 16]

    every = pl.ds(0, 4)
    whole = (pl.ds(0, HALF), pl.ds(HALF, HALF))
    part = (
        (pl.ds(0, FOLD), pl.ds(FOLD, FOLD)),
        (pl.ds(HALF, FOLD), pl.ds(HALF + FOLD, FOLD)),
    )

    def push(j, slot, ref, target):
        copy = pltpu.make_async_remote_copy(
            src_ref=ref,
            dst_ref=ref,
            send_sem=gsend.at[j, slot],
            recv_sem=grecv.at[j, slot],
            device_id=target,
            device_id_type=MESH,
        )
        copy.start()
        sends.append(copy)
        return copy

    right, left = (at(xr, y, z), at(x, yr, z)), (at(xl, y, z), at(x, yl, z))

    def line(j, half, xx, yy, columns):
        return rows.at[j, xx, yy, :, columns]

    def one(j):
        own = [line(j, h, x, y, whole[h]) for h in range(2)]
        return [push(j, 8 * h + d, own[h], (right, left)[d][h]) for d in range(2) for h in range(2)]

    def one_forward(j, got):
        copies = []
        for d in range(2):
            for h in range(2):
                got[2 * d + h].wait_recv()
                side = ((xl, yl), (xr, yr))[d]
                xx, yy = (side[0], y) if h == 0 else (x, side[1])
                ref = line(j, h, xx, yy, part[h][d])
                copies.append(push(j, 8 * h + 2 + d, ref, (right, left)[d][h]))
        return copies

    def two(j, got):
        for copy in got:
            copy.wait_recv()
        copies = []
        for d in range(2):
            for h in range(2):
                xx, yy = (every, y) if h == 0 else (x, every)
                ref = line(j, h, xx, yy, whole[h])
                copies.append(push(j, 8 * h + 4 + d, ref, (right, left)[d][1 - h]))
        return copies

    def two_forward(j, got):
        copies = []
        for d in range(2):
            for h in range(2):
                got[2 * d + h].wait_recv()
                side = ((xl, yl), (xr, yr))[d]
                xx, yy = (every, side[1]) if h == 0 else (side[0], every)
                ref = line(j, h, xx, yy, part[h][d])
                copies.append(push(j, 8 * h + 6 + d, ref, (right, left)[d][1 - h]))
        return copies

    def prepare(j):
        q = (quad + ORDER[j]) % 4

        @pl.loop(0, 16)
        def _(c):
            g = act[0, c, q].astype(F32)
            u = act[1, c, q].astype(F32)
            sig = 1.0 / (1.0 + jnp.exp(-g))
            gs = g * sig
            h = gs * u
            at_rows = pl.ds(pl.multiple_of(c * 16, 16), 16)
            hid[j, at_rows, :] = h
            cup[j, at_rows, :] = gs
            cgate[j, at_rows, :] = u * sig * (1.0 + g * (1.0 - sig))

        hidt[j] = hid[j].T.astype(BF16)

    def transpose_w():
        @pl.loop(0, D // 256)
        def _(k):
            at_cols = pl.ds(pl.multiple_of(k * 256, 256), 256)
            wt[at_cols, :] = w[:, at_cols].astype(F32).T.astype(BF16)

    stores = []

    def first_product(j):
        q = (quad + ORDER[j]) % 4
        d_out = jnp.dot(rows[j].reshape(256, D), wt[...], preferred_element_type=F32)
        dact[0, :, q] = (d_out * cgate[j]).astype(BF16).reshape(16, 16, 256)
        dact[1, :, q] = (d_out * cup[j]).astype(BF16).reshape(16, 16, 256)
        prod = d_out * hid[j]
        total = jnp.sum((prod[:, 0:128] + prod[:, 128:256]).T, axis=0, keepdims=True)
        psum[0, j : j + 1, :] = total[:, 0:128]
        psum[1, j : j + 1, :] = total[:, 128:256]
        store = pltpu.make_async_copy(
            dact.at[:, :, q], dact_hbm.at[:, :, q], local_sem.at[2 + j]
        )
        store.start()
        stores.append(store)

    def second_product(j, half):
        for k in range(3):
            out_cols = slice(k * 512, (k + 1) * 512)
            in_cols = pl.ds(pl.multiple_of(half * HALF + k * 512, 512), 512)
            block = rows[j, :, :, :, in_cols].reshape(256, 512)
            term = jnp.dot(hidt[j], block, preferred_element_type=F32)
            if j == 0:
                grad[half, :, out_cols] = term
            else:
                grad[half, :, out_cols] += term

    def compute(j):
        first_product(j)
        second_product(j, 0)
        second_product(j, 1)

    def landed(copies):
        for copy in copies:
            copy.wait_recv()

    assemble(0)
    a0 = one(0)
    load_act.wait()
    prepare(0)
    b0 = one_forward(0, a0)
    assemble(1)
    a1 = one(1)
    c0 = two(0, b0)
    b1 = one_forward(1, a1)
    load_w.wait()
    transpose_w()
    assemble(2)
    a2 = one(2)
    c1 = two(1, b1)
    prepare(1)
    d0 = two_forward(0, c0)
    b2 = one_forward(2, a2)
    assemble(3)
    a3 = one(3)
    c2 = two(2, b2)
    prepare(2)
    d1 = two_forward(1, c1)
    b3 = one_forward(3, a3)
    prepare(3)
    landed(d0)
    compute(0)
    c3 = two(3, b3)
    d2 = two_forward(2, c2)
    landed(d1)
    compute(1)
    d3 = two_forward(3, c3)
    landed(d2)
    compute(2)
    landed(d3)
    first_product(3)

    for k in range(1, 16):
        cc = (col + k) % 16
        copy = pltpu.make_async_remote_copy(
            src_ref=psum.at[cc // 8],
            dst_ref=psum_in.at[col],
            send_sem=psend.at[k - 1],
            recv_sem=precv,
            device_id=at_col(cc),
            device_id_type=MESH,
        )
        copy.start()
        sends.append(copy)
    psum_in[col] = psum[col // 8]

    second_product(3, 1 - p)
    swap = pltpu.make_async_remote_copy(
        src_ref=grad.at[1 - p],
        dst_ref=grad_in,
        send_sem=xsend,
        recv_sem=xrecv,
        device_id=sibling,
        device_id_type=MESH,
    )
    swap.start()
    second_product(3, p)

    arrived = psum_in.at[pl.ds(0, 15)]
    pltpu.make_async_copy(arrived, arrived, precv).wait()
    total = jnp.sum(psum_in[...], axis=0)
    for j in range(4):
        colsum[j] = total[j : j + 1]
    for k in range(1, 16):
        zz = (z + k) % 16
        rel = (zz // 4 - quad + 4) % 4
        j = jnp.where(rel == 3, 2, jnp.where(rel == 2, 3, rel))
        copy = pltpu.make_async_remote_copy(
            src_ref=colsum.at[j],
            dst_ref=colsum_in.at[z],
            send_sem=csend.at[k - 1],
            recv_sem=crecv,
            device_id=at(x, y, zz),
            device_id_type=MESH,
        )
        copy.start()
        sends.append(copy)
    colsum_in[z] = colsum[0]

    swap.wait_recv()
    for k in range(3):
        cols = slice(k * 512, (k + 1) * 512)
        dw[:, cols] = (grad[p, :, cols] + grad_in[:, cols]).astype(BF16)
    store_w = pltpu.make_async_copy(dw, dw_hbm, local_sem.at[6])
    store_w.start()

    arrived = colsum_in.at[pl.ds(0, 15)]
    pltpu.make_async_copy(arrived, arrived, crecv).wait()
    value = jnp.zeros((128, 128), F32)
    for i in range(8):
        both = colsum_in[i] + colsum_in[i + 8]
        value = jnp.where(row // 16 == i, both, value)
    mine = (col % 8) * 16 + (z % 4) * 4
    value = jnp.sum(jnp.where(lane == mine + row % 4, value, 0.0), axis=1, keepdims=True)
    for k, match in enumerate((first, second)):
        chosen = jnp.where(jnp.logical_and(hit, match), value, 0.0)
        score = jnp.sum(chosen, axis=0, keepdims=True) / gates[k : k + 1]
        droute_ref[k : k + 1, :] = score[:, 0:8]

    swap.wait_send()
    for copy in sends:
        copy.wait_send()
    for store in stores:
        store.wait()
    store_w.wait()


def per_device(out_grad, routes, route_weight, saved_act, w_down):
    vmem, hbm = pl.BlockSpec(memory_space=pltpu.VMEM), pl.BlockSpec(memory_space=pl.ANY)
    dma = pltpu.SemaphoreType.DMA
    d_act, d_weight, d_route = pl.pallas_call(
        kernel,
        out_shape=(
            jax.ShapeDtypeStruct((2, 16, 4, 16, 256), BF16),
            jax.ShapeDtypeStruct((256, HALF), BF16),
            jax.ShapeDtypeStruct((2, 8), F32),
        ),
        in_specs=[vmem, vmem, vmem, hbm, hbm],
        out_specs=(hbm, hbm, vmem),
        scratch_shapes=[
            pltpu.VMEM((2, 16, 4, 16, 256), BF16),
            pltpu.VMEM((256, D), BF16),
            pltpu.VMEM((D, 256), BF16),
            pltpu.VMEM((8, 16, FOLD), BF16),
            pltpu.VMEM((16, 16, FOLD), BF16),
            pltpu.VMEM((4, 4, 4, 16, D), BF16),
            pltpu.VMEM((4, 256, 256), F32),
            pltpu.VMEM((4, 256, 256), F32),
            pltpu.VMEM((4, 256, 256), F32),
            pltpu.VMEM((4, 256, 256), BF16),
            pltpu.VMEM((2, 16, 4, 16, 256), BF16),
            pltpu.VMEM((2, 256, HALF), F32),
            pltpu.VMEM((256, HALF), F32),
            pltpu.VMEM((256, HALF), BF16),
            pltpu.VMEM((2, 4, 128), F32),
            pltpu.VMEM((16, 4, 128), F32),
            pltpu.VMEM((4, 1, 128), F32),
            pltpu.VMEM((16, 1, 128), F32),
            dma((7,)),
            dma((15,)),
            dma((4,)),
            dma((4, 16)),
            dma((4, 16)),
            dma((15,)),
            dma,
            dma((15,)),
            dma,
            dma,
            dma,
        ],
        compiler_params=pltpu.CompilerParams(
            collective_id=0, has_side_effects=True, vmem_limit_bytes=48 * 1024 * 1024
        ),
    )(
        out_grad,
        routes.T,
        route_weight.T,
        saved_act.reshape(2, 16, 4, 16, 256),
        w_down[0],
    )
    return (
        d_act.reshape(saved_act.shape),
        d_weight[None],
        d_route.T,
    )


def solution(mesh):
    placed = (
        P(("expert", "etp", "dp"), None),
        P(("expert", "etp", "dp"), None),
        P(("expert", "etp", "dp"), None),
        P(None, "dp", "expert", None, "etp"),
        P("expert", "etp", None),
    )
    return jax.shard_map(
        per_device,
        mesh=mesh,
        in_specs=placed,
        out_specs=(
            P(None, "dp", "expert", None, "etp"),
            P("expert", "etp", "dp"),
            P(("expert", "etp", "dp"), None),
        ),
        check_vma=False,
    )
```

```python
import jax
import jax.numpy as jnp
from jax import lax
from jax.experimental import pallas as pl
from jax.experimental.pallas import tpu as pltpu
from jax.sharding import PartitionSpec as P

MESH = pl.DeviceIdType.MESH
F32 = jnp.float32
BF16 = jnp.bfloat16
D = 3072
HALF = D // 2
FOLD = D // 4
NEAR = ((0, 1, 15, 2), (14, 13, 3, 4), (12, 11, 5, 6), (10, 9, 7, 8))


def iota(shape, axis):
    return lax.broadcasted_iota(jnp.int32, shape, axis)


def kernel(
    tok_hbm, route_hbm, weight_hbm, act_hbm, w_hbm,
    dact, dw, droute,
    tok_ref, route_ref, weight_ref, act, w, wt, outgoing, zbuf, rows, hid, cgate, cup, hidt, drel, grad, grad_in,
    last, last_in, psum, psum_in, colsum, colsum_in,
    local_sem, zsend, zrecv, gsend, grecv, psend, precv, csend, crecv, xsend, xrecv,
):
    e = lax.axis_index("expert")
    t = lax.axis_index("etp")
    p = lax.axis_index("dp")
    x, y, zh = t // 8, (t // 2) % 4, t % 2
    z = zh * 8 + e
    col = x * 4 + y

    def at(xx, yy, zz):
        return (zz % 8, xx * 8 + yy * 2 + zz // 8, p)

    def at_col(cc):
        return at(cc // 4, cc % 4, z)

    sibling = (e, t, 1 - p)
    xr, xl, yr, yl = (x + 1) % 4, (x + 3) % 4, (y + 1) % 4, (y + 3) % 4

    loads = []
    for k, (src, dst) in enumerate(
        ((route_hbm, route_ref), (weight_hbm, weight_ref), (tok_hbm, tok_ref), (act_hbm, act), (w_hbm, w))
    ):
        loads.append(pltpu.make_async_copy(src, dst, local_sem.at[k]))
        loads[k].start()
    load_act, load_w = loads[3:]

    barrier = pltpu.get_barrier_semaphore()
    for k in range(1, 16):
        pl.semaphore_signal(barrier, inc=1, device_id=at(x, y, (z + k) % 16), device_id_type=MESH)
        pl.semaphore_signal(barrier, inc=1, device_id=at_col((col + k) % 16), device_id_type=MESH)
    pl.semaphore_signal(barrier, inc=1, device_id=sibling, device_id_type=MESH)

    spread = (iota((8, 128), 1) % 8 == iota((8, 128), 0)).astype(BF16)
    for k in range(3):
        loads[k].wait()
    routes = jnp.dot(route_ref[...].astype(F32).astype(BF16), spread, preferred_element_type=F32)
    gates = jnp.dot(weight_ref[...], spread, preferred_element_type=F32)
    row, lane = iota((128, 128), 0), iota((128, 128), 1)
    row_e = (row // 16).astype(F32)
    first, second = routes[0:1] == row_e, routes[1:2] == row_e
    named = jnp.logical_or(first, second)
    earlier = jnp.logical_and(row // 8 == lane // 8, row < lane).astype(BF16)
    rank = jnp.dot(named.astype(F32).astype(BF16), earlier, preferred_element_type=F32)
    hit = jnp.logical_and(named, rank == (row % 4).astype(F32))
    hit = jnp.logical_and(hit, (row // 4) % 4 == lane // 8)
    pick = jnp.where(hit, jnp.where(first, gates[0:1], gates[1:2]), 0.0).astype(BF16)
    token = tok_ref[...].astype(F32)
    folded = jnp.concatenate([token[:, i * FOLD : (i + 1) * FOLD] for i in range(4)], axis=0)
    slots = jnp.dot(pick[:, 0:32], folded.astype(BF16), preferred_element_type=F32)
    outgoing[...] = slots.astype(BF16).reshape(8, 16, FOLD)

    pl.semaphore_wait(barrier, 31)

    sends = []

    def along(j):
        for k, near in enumerate(NEAR[j]):
            if near == 0:
                continue
            zz = (z + 16 - near) % 16
            copy = pltpu.make_async_remote_copy(
                src_ref=outgoing.at[zz % 8],
                dst_ref=zbuf.at[j, k],
                send_sem=zsend.at[j, k],
                recv_sem=zrecv.at[j],
                device_id=at(x, y, zz),
                device_id_type=MESH,
            )
            copy.start()
            sends.append(copy)

    along(0)
    along(1)
    zbuf[0, 0] = outgoing[e]

    mrow, mcol = iota((64, 64), 0), iota((64, 64), 1)
    unfold = jnp.logical_and(mrow // 16 == (mcol // 4) % 4, (mrow // 4) % 4 == mcol // 16)
    unfold = jnp.logical_and(unfold, mrow % 4 == mcol % 4).astype(F32).astype(BF16)

    def assemble(j):
        landed = zbuf.at[j, pl.ds(1, 3)] if j == 0 else zbuf.at[j]
        pltpu.make_async_copy(landed, landed, zrecv.at[j]).wait()
        block = zbuf[j].reshape(64, FOLD)
        flat = jnp.dot(unfold, block, preferred_element_type=F32).astype(BF16)
        for i in range(4):
            rows[j, x, y, :, i * FOLD : (i + 1) * FOLD] = flat[i * 16 : (i + 1) * 16]

    every = pl.ds(0, 4)
    whole = (pl.ds(0, HALF), pl.ds(HALF, HALF))
    part = (
        (pl.ds(0, FOLD), pl.ds(FOLD, FOLD)),
        (pl.ds(HALF, FOLD), pl.ds(HALF + FOLD, FOLD)),
    )

    def push(j, slot, ref, target):
        copy = pltpu.make_async_remote_copy(
            src_ref=ref,
            dst_ref=ref,
            send_sem=gsend.at[j, slot],
            recv_sem=grecv.at[j, slot],
            device_id=target,
            device_id_type=MESH,
        )
        copy.start()
        sends.append(copy)
        return copy

    right, left = (at(xr, y, z), at(x, yr, z)), (at(xl, y, z), at(x, yl, z))
    across = (at((x + 2) % 4, y, z), at(x, (y + 2) % 4, z))

    def line(j, half, xx, yy, columns):
        return rows.at[j, xx, yy, :, columns]

    def one(j):
        copies = []
        for d, target in enumerate((across, right, left)):
            for h in range(2):
                copies.append(push(j, 9 * h + d, line(j, h, x, y, whole[h]), target[h]))
        return copies

    def two(j, got):
        for copy in got:
            copy.wait_recv()
        copies = []
        for i in range(2):
            for d in range(2):
                for h in range(2):
                    xx, yy = (every, y) if h == 0 else (x, every)
                    ref = line(j, h, xx, yy, part[h][d if i == 0 else 1 - d])
                    copies.append(push(j, 9 * h + 3 + 2 * i + d, ref, (right, left)[d][1 - h]))
        return copies

    def onward(j, got):
        copies = []
        for d in range(2):
            for h in range(2):
                got[2 * d + h].wait_recv()
                side = ((xl, yl), (xr, yr))[d]
                xx, yy = (every, side[1]) if h == 0 else (side[0], every)
                ref = line(j, h, xx, yy, part[h][d])
                copies.append(push(j, 9 * h + 7 + d, ref, (right, left)[d][1 - h]))
        return copies + got[4:]

    frow, fcol = iota((64, 64), 0), iota((64, 64), 1)

    def chunked(place):
        near = jnp.zeros((64, 64), jnp.int32)
        for k, value in enumerate(sum(NEAR, ())):
            near = jnp.where(place // 4 == k, value, near)
        return 4 * ((z + near) % 16) + place % 4

    gather = (fcol == chunked(frow)).astype(F32).astype(BF16)
    scatter = (frow == chunked(fcol)).astype(F32).astype(BF16)

    def prepare(part):
        @pl.loop(part * 4, part * 4 + 4)
        def _(c):
            g = jnp.dot(gather, act[0, c], preferred_element_type=F32)
            u = jnp.dot(gather, act[1, c], preferred_element_type=F32)
            sig = 1.0 / (1.0 + jnp.exp(-g))
            gs = g * sig
            h = gs * u
            slope = u * sig * (1.0 + g * (1.0 - sig))
            at_rows = pl.ds(pl.multiple_of(c * 16, 16), 16)
            for j in range(4):
                mine = slice(j * 16, (j + 1) * 16)
                hid[j, at_rows, :] = h[mine]
                cup[j, at_rows, :] = gs[mine]
                cgate[j, at_rows, :] = slope[mine]

    def flip():
        for j in range(4):
            hidt[j] = hid[j].T.astype(BF16)

    def transpose_w():
        @pl.loop(0, D // 256)
        def _(k):
            at_cols = pl.ds(pl.multiple_of(k * 256, 256), 256)
            wt[at_cols, :] = w[:, at_cols].astype(F32).T.astype(BF16)

    def first_product(j):
        d_out = jnp.dot(rows[j].reshape(256, D), wt[...], preferred_element_type=F32)
        prod = d_out * hid[j]
        total = jnp.sum((prod[:, 0:128] + prod[:, 128:256]).T, axis=0, keepdims=True)
        psum[0, j, :, :] = total[:, 0:128]
        psum[1, j, :, :] = total[:, 128:256]
        return d_out

    def slopes(j, d_out):
        drel[0, :, j] = (d_out * cgate[j]).astype(BF16).reshape(16, 16, 256)
        drel[1, :, j] = (d_out * cup[j]).astype(BF16).reshape(16, 16, 256)

    def second_product(j, half, store):
        for k in range(3):
            in_cols = pl.ds(pl.multiple_of(half * HALF + k * 512, 512), 512)
            block = rows[j, :, :, :, in_cols].reshape(256, 512)
            store(slice(k * 512, (k + 1) * 512), jnp.dot(hidt[j], block, preferred_element_type=F32))

    def compute(j):
        slopes(j, first_product(j))
        for half in range(2):

            def store(cols, term):
                grad[half, :, cols] = term if j == 0 else grad[half, :, cols] + term

            second_product(j, half, store)

    def to_columns(js):
        for k in range(1, 16):
            cc = (col + k) % 16
            copy = pltpu.make_async_remote_copy(
                src_ref=psum.at[cc // 8, js],
                dst_ref=psum_in.at[col, js],
                send_sem=psend.at[js.start // 3, k - 1],
                recv_sem=precv.at[js.start // 3],
                device_id=at_col(cc),
                device_id_type=MESH,
            )
            copy.start()
            sends.append(copy)
        psum_in[col, js] = psum[col // 8, js]

    def along_column(js):
        arrived = psum_in.at[pl.ds(0, 15), js]
        pltpu.make_async_copy(arrived, arrived, precv.at[js.start // 3]).wait()
        for j in range(js.start, js.start + js.size):
            total = jnp.sum(psum_in[:, j], axis=0)
            for k, near in enumerate(NEAR[j]):
                turned = total if k == 0 else jnp.concatenate([total[:, 4 * k :], total[:, : 4 * k]], axis=1)
                colsum[j, k] = turned
                if near == 0:
                    colsum_in[z] = turned
                    continue
                copy = pltpu.make_async_remote_copy(
                    src_ref=colsum.at[j, k],
                    dst_ref=colsum_in.at[z],
                    send_sem=csend.at[j, k],
                    recv_sem=crecv,
                    device_id=at(x, y, (z + near) % 16),
                    device_id_type=MESH,
                )
                copy.start()
                sends.append(copy)

    def landed(copies):
        for copy in copies:
            copy.wait_recv()

    assemble(0)
    a0 = one(0)
    along(2)
    along(3)
    load_act.wait()
    prepare(0)
    prepare(1)
    b0 = two(0, a0)
    assemble(1)
    a1 = one(1)
    prepare(2)
    c0 = onward(0, b0)
    prepare(3)
    b1 = two(1, a1)
    load_w.wait()
    transpose_w()
    flip()
    assemble(2)
    a2 = one(2)
    c1 = onward(1, b1)
    landed(c0)
    compute(0)
    b2 = two(2, a2)
    assemble(3)
    a3 = one(3)
    c2 = onward(2, b2)
    landed(c1)
    compute(1)
    b3 = two(3, a3)
    landed(c2)
    compute(2)
    c3 = onward(3, b3)

    def to_sibling(i, src, dst):
        copy = pltpu.make_async_remote_copy(
            src_ref=src, dst_ref=dst, send_sem=xsend.at[i], recv_sem=xrecv.at[i], device_id=sibling, device_id_type=MESH
        )
        copy.start()
        sends.append(copy)
        return copy

    for copy in sends[:-22]:
        copy.wait_send()
    sends = sends[-22:]
    most = to_sibling(0, grad.at[1 - p], grad_in)
    to_columns(pl.ds(0, 3))
    landed(c3)
    d_out = first_product(3)
    to_columns(pl.ds(3, 1))

    def store_last(cols, term):
        last[:, cols] = term.astype(BF16)

    def store_grad(cols, term):
        grad[p, :, cols] += term

    second_product(3, 1 - p, store_last)
    rest = to_sibling(1, last, last_in)
    along_column(pl.ds(0, 3))
    slopes(3, d_out)
    along_column(pl.ds(3, 1))
    second_product(3, p, store_grad)
    for i in range(2):
        for c in range(16):
            dact[i, c] = jnp.dot(scatter, drel[i, c].reshape(64, 256), preferred_element_type=F32).astype(BF16)

    most.wait_recv()
    rest.wait_recv()
    for k in range(3):
        cols = slice(k * 512, (k + 1) * 512)
        dw[:, cols] = (grad[p, :, cols] + grad_in[:, cols] + last_in[:, cols].astype(F32)).astype(BF16)
    arrived = colsum_in.at[pl.ds(0, 15)]
    pltpu.make_async_copy(arrived, arrived, crecv).wait()
    value = jnp.zeros((128, 128), F32)
    for i in range(8):
        both = colsum_in[i] + colsum_in[i + 8]
        value = jnp.where(row // 16 == i, both, value)
    mine = (col % 8) * 16
    value = jnp.sum(jnp.where(lane == mine + row % 4, value, 0.0), axis=1, keepdims=True)
    for k, match in enumerate((first, second)):
        chosen = jnp.where(jnp.logical_and(hit, match), value, 0.0)
        score = jnp.sum(chosen, axis=0, keepdims=True) / gates[k : k + 1]
        droute[k : k + 1, :] = score[:, 0:8]
    for copy in sends:
        copy.wait_send()


def finish(dact_in, dw_in, droute_in, dact, dw, droute, sem):
    copies = [pltpu.make_async_copy(dw_in, dw, sem.at[0]), pltpu.make_async_copy(droute_in, droute, sem.at[1])]
    for i in range(4):
        quarter = pl.ds(4 * i, 4)
        copies.append(pltpu.make_async_copy(dact_in.at[:, quarter], dact.at[:, quarter], sem.at[2 + i]))
    for copy in copies:
        copy.start()
    for copy in copies:
        copy.wait()


def per_device(out_grad, routes, route_weight, saved_act, w_down):
    hbm, anywhere = pl.BlockSpec(memory_space=pltpu.HBM), pl.BlockSpec(memory_space=pl.ANY)
    shapes = (
        jax.ShapeDtypeStruct((2, 16, 64, 256), BF16),
        jax.ShapeDtypeStruct((256, HALF), BF16),
        jax.ShapeDtypeStruct((2, 8), F32),
    )
    dma = pltpu.SemaphoreType.DMA
    results = pl.pallas_call(
        kernel,
        out_shape=shapes,
        in_specs=[hbm] * 5,
        out_specs=(pl.BlockSpec(memory_space=pltpu.VMEM),) * 3,
        scratch_shapes=[
            pltpu.VMEM((8, D), BF16),
            pltpu.VMEM((2, 8), jnp.int32),
            pltpu.VMEM((2, 8), BF16),
            pltpu.VMEM((2, 16, 64, 256), BF16),
            pltpu.VMEM((256, D), BF16),
            pltpu.VMEM((D, 256), BF16),
            pltpu.VMEM((8, 16, FOLD), BF16),
            pltpu.VMEM((4, 4, 16, FOLD), BF16),
            pltpu.VMEM((4, 4, 4, 16, D), BF16),
            pltpu.VMEM((4, 256, 256), F32),
            pltpu.VMEM((4, 256, 256), F32),
            pltpu.VMEM((4, 256, 256), F32),
            pltpu.VMEM((4, 256, 256), BF16),
            pltpu.VMEM((2, 16, 4, 16, 256), BF16),
            pltpu.VMEM((2, 256, HALF), F32),
            pltpu.VMEM((256, HALF), F32),
            pltpu.VMEM((256, HALF), BF16),
            pltpu.VMEM((256, HALF), BF16),
            pltpu.VMEM((2, 4, 1, 128), F32),
            pltpu.VMEM((16, 4, 1, 128), F32),
            pltpu.VMEM((4, 4, 1, 128), F32),
            pltpu.VMEM((16, 1, 128), F32),
            dma((5,)),
            dma((4, 4)),
            dma((4,)),
            dma((4, 18)),
            dma((4, 18)),
            dma((2, 15)),
            dma((2,)),
            dma((4, 4)),
            dma,
            dma((2,)),
            dma((2,)),
        ],
        compiler_params=pltpu.CompilerParams(
            collective_id=0, has_side_effects=True, vmem_limit_bytes=40 * 1024 * 1024
        ),
    )(
        *(
            pltpu.with_memory_space_constraint(value, pltpu.HBM)
            for value in (out_grad, routes.T, route_weight.T, saved_act.reshape(2, 16, 64, 256), w_down[0])
        )
    )
    d_act, d_weight, d_route = pl.pallas_call(
        finish,
        out_shape=shapes,
        in_specs=[anywhere] * 3,
        out_specs=(hbm,) * 3,
        scratch_shapes=[dma((6,))],
        compiler_params=pltpu.CompilerParams(vmem_limit_bytes=2 * 1024 * 1024),
    )(*results)
    return (
        d_act.reshape(saved_act.shape),
        d_weight[None],
        d_route.T,
    )


def solution(mesh):
    placed = (
        P(("expert", "etp", "dp"), None),
        P(("expert", "etp", "dp"), None),
        P(("expert", "etp", "dp"), None),
        P(None, "dp", "expert", None, "etp"),
        P("expert", "etp", None),
    )
    return jax.shard_map(
        per_device,
        mesh=mesh,
        in_specs=placed,
        out_specs=(
            P(None, "dp", "expert", None, "etp"),
            P("expert", "etp", "dp"),
            P(("expert", "etp", "dp"), None),
        ),
        check_vma=False,
    )
```

```python
import jax
import jax.numpy as jnp
from jax import lax
from jax.experimental import pallas as pl
from jax.experimental.pallas import tpu as pltpu
from jax.sharding import PartitionSpec as P

MESH = pl.DeviceIdType.MESH
F32 = jnp.float32
BF16 = jnp.bfloat16
D = 3072
HALF = D // 2
FOLD = D // 4
NEAR = ((0, 1, 15, 2), (14, 13, 3, 4), (12, 11, 5, 6), (10, 9, 7, 8))


def iota(shape, axis):
    return lax.broadcasted_iota(jnp.int32, shape, axis)


def kernel(
    tok_hbm, route_hbm, weight_hbm, act_hbm, w_hbm,
    dact, dw, droute,
    tok_ref, route_ref, weight_ref, act, w, wt, outgoing, zbuf, rows, hid, cgate, cup, hidt, drel, grad, grad_in,
    last, last_in, psum, psum_in, colsum, colsum_in, late_in,
    local_sem, zsend, zrecv, gsend, grecv, psend, precv, csend, crecv, lsend, lrecv, xsend, xrecv, far_sem,
):
    e = lax.axis_index("expert")
    t = lax.axis_index("etp")
    p = lax.axis_index("dp")
    x, y, zh = t // 8, (t // 2) % 4, t % 2
    z = zh * 8 + e
    col = x * 4 + y

    def at(xx, yy, zz):
        return (zz % 8, xx * 8 + yy * 2 + zz // 8, p)

    def at_col(cc):
        return at(cc // 4, cc % 4, z)

    sibling = (e, t, 1 - p)
    xr, xl, yr, yl = (x + 1) % 4, (x + 3) % 4, (y + 1) % 4, (y + 3) % 4

    loads = []
    for k, (src, dst) in enumerate(
        ((route_hbm, route_ref), (weight_hbm, weight_ref), (tok_hbm, tok_ref), (act_hbm, act), (w_hbm, w))
    ):
        loads.append(pltpu.make_async_copy(src, dst, local_sem.at[k]))
        loads[k].start()
    load_act, load_w = loads[3:]

    barrier = pltpu.get_barrier_semaphore()
    near = [at(x, y, (z + k) % 16) for k in (1, 15, 2, 14)]
    near += [at((x + k) % 4, y, z) for k in (1, 3, 2)] + [at(x, (y + k) % 4, z) for k in (1, 3, 2)] + [sibling]
    for device in near:
        pl.semaphore_signal(barrier, inc=1, device_id=device, device_id_type=MESH)

    def tell(i):
        for k in (2 << i, 16 - (2 << i)):
            pl.semaphore_signal(far_sem.at[i], inc=1, device_id=at(x, y, (z + k) % 16), device_id_type=MESH)

    spread = (iota((8, 128), 1) % 8 == iota((8, 128), 0)).astype(BF16)
    for k in range(3):
        loads[k].wait()
    routes = jnp.dot(route_ref[...].astype(F32).astype(BF16), spread, preferred_element_type=F32)
    gates = jnp.dot(weight_ref[...], spread, preferred_element_type=F32)
    row, lane = iota((128, 128), 0), iota((128, 128), 1)
    row_e = (row // 16).astype(F32)
    first, second = routes[0:1] == row_e, routes[1:2] == row_e
    named = jnp.logical_or(first, second)
    earlier = jnp.logical_and(row // 8 == lane // 8, row < lane).astype(BF16)
    rank = jnp.dot(named.astype(F32).astype(BF16), earlier, preferred_element_type=F32)
    hit = jnp.logical_and(named, rank == (row % 4).astype(F32))
    hit = jnp.logical_and(hit, (row // 4) % 4 == lane // 8)
    pick = jnp.where(hit, jnp.where(first, gates[0:1], gates[1:2]), 0.0).astype(BF16)
    token = tok_ref[...].astype(F32)
    folded = jnp.concatenate([token[:, i * FOLD : (i + 1) * FOLD] for i in range(4)], axis=0)
    slots = jnp.dot(pick[:, 0:32], folded.astype(BF16), preferred_element_type=F32)
    outgoing[...] = slots.astype(BF16).reshape(8, 16, FOLD)

    pl.semaphore_wait(barrier, len(near))

    sends = []

    def along(j):
        for k, near in enumerate(NEAR[j]):
            if near == 0:
                continue
            zz = (z + 16 - near) % 16
            copy = pltpu.make_async_remote_copy(
                src_ref=outgoing.at[zz % 8],
                dst_ref=zbuf.at[j, k],
                send_sem=zsend.at[j, k],
                recv_sem=zrecv.at[j],
                device_id=at(x, y, zz),
                device_id_type=MESH,
            )
            copy.start()
            sends.append(copy)

    along(0)
    tell(0)
    zbuf[0, 0] = outgoing[e]

    mrow, mcol = iota((64, 64), 0), iota((64, 64), 1)
    unfold = jnp.logical_and(mrow // 16 == (mcol // 4) % 4, (mrow // 4) % 4 == mcol // 16)
    unfold = jnp.logical_and(unfold, mrow % 4 == mcol % 4).astype(F32).astype(BF16)

    def assemble(j):
        landed = zbuf.at[j, pl.ds(1, 3)] if j == 0 else zbuf.at[j]
        pltpu.make_async_copy(landed, landed, zrecv.at[j]).wait()
        block = zbuf[j].reshape(64, FOLD)
        flat = jnp.dot(unfold, block, preferred_element_type=F32).astype(BF16)
        for i in range(4):
            rows[j, x, y, :, i * FOLD : (i + 1) * FOLD] = flat[i * 16 : (i + 1) * 16]

    every = pl.ds(0, 4)
    whole = (pl.ds(0, HALF), pl.ds(HALF, HALF))
    part = (
        (pl.ds(0, FOLD), pl.ds(FOLD, FOLD)),
        (pl.ds(HALF, FOLD), pl.ds(HALF + FOLD, FOLD)),
    )

    def push(j, slot, ref, target):
        copy = pltpu.make_async_remote_copy(
            src_ref=ref,
            dst_ref=ref,
            send_sem=gsend.at[j, slot],
            recv_sem=grecv.at[j, slot],
            device_id=target,
            device_id_type=MESH,
        )
        copy.start()
        sends.append(copy)
        return copy

    right, left = (at(xr, y, z), at(x, yr, z)), (at(xl, y, z), at(x, yl, z))
    across = (at((x + 2) % 4, y, z), at(x, (y + 2) % 4, z))

    def line(j, half, xx, yy, columns):
        return rows.at[j, xx, yy, :, columns]

    def one(j):
        copies = []
        for d, target in enumerate((across, right, left)):
            for h in range(2):
                copies.append(push(j, 9 * h + d, line(j, h, x, y, whole[h]), target[h]))
        return copies

    def two(j, got):
        for copy in got:
            copy.wait_recv()
        copies = []
        for i in range(2):
            for d in range(2):
                for h in range(2):
                    xx, yy = (every, y) if h == 0 else (x, every)
                    ref = line(j, h, xx, yy, part[h][d if i == 0 else 1 - d])
                    copies.append(push(j, 9 * h + 3 + 2 * i + d, ref, (right, left)[d][1 - h]))
        return copies

    def onward(j, got):
        copies = []
        for d in range(2):
            for h in range(2):
                got[2 * d + h].wait_recv()
                side = ((xl, yl), (xr, yr))[d]
                xx, yy = (every, side[1]) if h == 0 else (side[0], every)
                ref = line(j, h, xx, yy, part[h][d])
                copies.append(push(j, 9 * h + 7 + d, ref, (right, left)[d][1 - h]))
        return copies + got[4:]

    frow, fcol = iota((64, 64), 0), iota((64, 64), 1)

    def chunked(place):
        near = jnp.zeros((64, 64), jnp.int32)
        for k, value in enumerate(sum(NEAR, ())):
            near = jnp.where(place // 4 == k, value, near)
        return 4 * ((z + near) % 16) + place % 4

    gather = (fcol == chunked(frow)).astype(F32).astype(BF16)
    scatter = (frow == chunked(fcol)).astype(F32).astype(BF16)

    def prepare(part):
        @pl.loop(part * 4, part * 4 + 4)
        def _(c):
            g = jnp.dot(gather, act[0, c], preferred_element_type=F32)
            u = jnp.dot(gather, act[1, c], preferred_element_type=F32)
            sig = 1.0 / (1.0 + jnp.exp(-g))
            gs = g * sig
            h = gs * u
            slope = u * sig * (1.0 + g * (1.0 - sig))
            at_rows = pl.ds(pl.multiple_of(c * 16, 16), 16)
            for j in range(4):
                mine = slice(j * 16, (j + 1) * 16)
                hid[j, at_rows, :] = h[mine]
                cup[j, at_rows, :] = gs[mine]
                cgate[j, at_rows, :] = slope[mine]

    def flip():
        for j in range(4):
            hidt[j] = hid[j].T.astype(BF16)

    def transpose_w():
        @pl.loop(0, D // 256)
        def _(k):
            at_cols = pl.ds(pl.multiple_of(k * 256, 256), 256)
            wt[at_cols, :] = w[:, at_cols].astype(F32).T.astype(BF16)

    def first_product(j):
        d_out = jnp.dot(rows[j].reshape(256, D), wt[...], preferred_element_type=F32)
        prod = d_out * hid[j]
        total = jnp.sum((prod[:, 0:128] + prod[:, 128:256]).T, axis=0, keepdims=True)
        psum[0, j, :, :] = total[:, 0:128]
        psum[1, j, :, :] = total[:, 128:256]
        return d_out

    def slopes(j, d_out):
        drel[0, :, j] = (d_out * cgate[j]).astype(BF16).reshape(16, 16, 256)
        drel[1, :, j] = (d_out * cup[j]).astype(BF16).reshape(16, 16, 256)

    def second_product(j, half, store):
        for k in range(3):
            in_cols = pl.ds(pl.multiple_of(half * HALF + k * 512, 512), 512)
            block = rows[j, :, :, :, in_cols].reshape(256, 512)
            store(slice(k * 512, (k + 1) * 512), jnp.dot(hidt[j], block, preferred_element_type=F32))

    def compute(j):
        slopes(j, first_product(j))
        for half in range(2):

            def store(cols, term):
                grad[half, :, cols] = term if j == 0 else grad[half, :, cols] + term

            second_product(j, half, store)

    early = pl.ds(0, 2)

    def to_columns():
        for k in range(1, 16):
            cc = (col + k) % 16
            copy = pltpu.make_async_remote_copy(
                src_ref=psum.at[cc // 8, early],
                dst_ref=psum_in.at[col],
                send_sem=psend.at[k - 1],
                recv_sem=precv,
                device_id=at_col(cc),
                device_id_type=MESH,
            )
            copy.start()
            sends.append(copy)
        psum_in[col] = psum[col // 8, early]

    def along_column():
        arrived = psum_in.at[pl.ds(0, 15)]
        pltpu.make_async_copy(arrived, arrived, precv).wait()
        for j in range(2):
            total = jnp.sum(psum_in[:, j], axis=0)
            for k, near in enumerate(NEAR[j]):
                turned = total if k == 0 else jnp.concatenate([total[:, 4 * k :], total[:, : 4 * k]], axis=1)
                colsum[j, k] = turned
                if near == 0:
                    colsum_in[z] = turned
                    continue
                copy = pltpu.make_async_remote_copy(
                    src_ref=colsum.at[j, k],
                    dst_ref=colsum_in.at[z],
                    send_sem=csend.at[j, k],
                    recv_sem=crecv,
                    device_id=at(x, y, (z + near) % 16),
                    device_id_type=MESH,
                )
                copy.start()
                sends.append(copy)

    def to_tokens(j):
        for i in range(16):
            cc = (col + 15 - i) % 16
            for k, near in enumerate(NEAR[j]):
                copy = pltpu.make_async_remote_copy(
                    src_ref=psum.at[cc // 8, j],
                    dst_ref=late_in.at[j - 2, k, col],
                    send_sem=lsend.at[j - 2],
                    recv_sem=lrecv.at[j - 2],
                    device_id=(
                        (z + near) % 8,
                        (cc // 4) * 8 + (cc % 4) * 2 + ((z + near) % 16) // 8,
                        p,
                    ),
                    device_id_type=MESH,
                )
                copy.start()

    def landed(copies):
        for copy in copies:
            copy.wait_recv()

    pl.semaphore_wait(far_sem.at[0], 2)
    tell(1)
    along(1)
    assemble(0)
    a0 = one(0)
    pl.semaphore_wait(far_sem.at[1], 2)
    along(2)
    along(3)
    load_act.wait()
    prepare(0)
    prepare(1)
    b0 = two(0, a0)
    assemble(1)
    a1 = one(1)
    prepare(2)
    c0 = onward(0, b0)
    prepare(3)
    b1 = two(1, a1)
    load_w.wait()
    transpose_w()
    flip()
    assemble(2)
    a2 = one(2)
    c1 = onward(1, b1)
    landed(c0)
    compute(0)
    b2 = two(2, a2)
    assemble(3)
    a3 = one(3)
    c2 = onward(2, b2)
    landed(c1)
    compute(1)
    to_columns()
    b3 = two(3, a3)
    landed(c2)
    compute(2)
    c3 = onward(3, b3)
    to_tokens(2)
    along_column()

    def to_sibling(i, src, dst):
        copy = pltpu.make_async_remote_copy(
            src_ref=src, dst_ref=dst, send_sem=xsend.at[i], recv_sem=xrecv.at[i], device_id=sibling, device_id_type=MESH
        )
        copy.start()
        sends.append(copy)
        return copy

    under_way = len(sends) - 18 - 15 - 7
    for copy in sends[:under_way]:
        copy.wait_send()
    sends = sends[under_way:]
    most = to_sibling(0, grad.at[1 - p], grad_in)
    landed(c3)
    d_out = first_product(3)
    to_tokens(3)

    def store_last(cols, term):
        last[:, cols] = term.astype(BF16)

    def store_grad(cols, term):
        grad[p, :, cols] += term

    second_product(3, 1 - p, store_last)
    rest = to_sibling(1, last, last_in)
    slopes(3, d_out)
    second_product(3, p, store_grad)
    for i in range(2):
        for c in range(16):
            dact[i, c] = jnp.dot(scatter, drel[i, c].reshape(64, 256), preferred_element_type=F32).astype(BF16)

    most.wait_recv()
    rest.wait_recv()
    for k in range(3):
        cols = slice(k * 512, (k + 1) * 512)
        dw[:, cols] = (grad[p, :, cols] + grad_in[:, cols] + last_in[:, cols].astype(F32)).astype(BF16)
    arrived = colsum_in.at[pl.ds(0, 7)]
    pltpu.make_async_copy(arrived, arrived, crecv).wait()
    for j in (2, 3):
        late = late_in.at[j - 2]
        pltpu.make_async_copy(late, late, lrecv.at[j - 2]).wait()
        for k, near in enumerate(NEAR[j]):
            total = jnp.sum(late_in[j - 2, k], axis=0)
            turned = total if k == 0 else jnp.concatenate([total[:, 4 * k :], total[:, : 4 * k]], axis=1)
            colsum_in[(z + 16 - near) % 16] = turned
    value = jnp.zeros((128, 128), F32)
    for i in range(8):
        both = colsum_in[i] + colsum_in[i + 8]
        value = jnp.where(row // 16 == i, both, value)
    mine = (col % 8) * 16
    value = jnp.sum(jnp.where(lane == mine + row % 4, value, 0.0), axis=1, keepdims=True)
    for k, match in enumerate((first, second)):
        chosen = jnp.where(jnp.logical_and(hit, match), value, 0.0)
        score = jnp.sum(chosen, axis=0, keepdims=True) / gates[k : k + 1]
        droute[k : k + 1, :] = score[:, 0:8]
    for copy in sends:
        copy.wait_send()
    for i in range(2):
        pltpu.make_async_copy(late_in.at[i], late_in.at[i], lsend.at[i]).wait()


def finish(dact_in, dw_in, droute_in, dact, dw, droute, sem):
    copies = [pltpu.make_async_copy(dw_in, dw, sem.at[0]), pltpu.make_async_copy(droute_in, droute, sem.at[1])]
    for i in range(4):
        quarter = pl.ds(4 * i, 4)
        copies.append(pltpu.make_async_copy(dact_in.at[:, quarter], dact.at[:, quarter], sem.at[2 + i]))
    for copy in copies:
        copy.start()
    for copy in copies:
        copy.wait()


def per_device(out_grad, routes, route_weight, saved_act, w_down):
    hbm, anywhere = pl.BlockSpec(memory_space=pltpu.HBM), pl.BlockSpec(memory_space=pl.ANY)
    shapes = (
        jax.ShapeDtypeStruct((2, 16, 64, 256), BF16),
        jax.ShapeDtypeStruct((256, HALF), BF16),
        jax.ShapeDtypeStruct((2, 8), F32),
    )
    dma = pltpu.SemaphoreType.DMA
    results = pl.pallas_call(
        kernel,
        out_shape=shapes,
        in_specs=[hbm] * 5,
        out_specs=(pl.BlockSpec(memory_space=pltpu.VMEM),) * 3,
        scratch_shapes=[
            pltpu.VMEM((8, D), BF16),
            pltpu.VMEM((2, 8), jnp.int32),
            pltpu.VMEM((2, 8), BF16),
            pltpu.VMEM((2, 16, 64, 256), BF16),
            pltpu.VMEM((256, D), BF16),
            pltpu.VMEM((D, 256), BF16),
            pltpu.VMEM((8, 16, FOLD), BF16),
            pltpu.VMEM((4, 4, 16, FOLD), BF16),
            pltpu.VMEM((4, 4, 4, 16, D), BF16),
            pltpu.VMEM((4, 256, 256), F32),
            pltpu.VMEM((4, 256, 256), F32),
            pltpu.VMEM((4, 256, 256), F32),
            pltpu.VMEM((4, 256, 256), BF16),
            pltpu.VMEM((2, 16, 4, 16, 256), BF16),
            pltpu.VMEM((2, 256, HALF), F32),
            pltpu.VMEM((256, HALF), F32),
            pltpu.VMEM((256, HALF), BF16),
            pltpu.VMEM((256, HALF), BF16),
            pltpu.VMEM((2, 4, 1, 128), F32),
            pltpu.VMEM((16, 2, 1, 128), F32),
            pltpu.VMEM((2, 4, 1, 128), F32),
            pltpu.VMEM((16, 1, 128), F32),
            pltpu.VMEM((2, 4, 16, 1, 128), F32),
            dma((5,)),
            dma((4, 4)),
            dma((4,)),
            dma((4, 18)),
            dma((4, 18)),
            dma((15,)),
            dma,
            dma((2, 4)),
            dma,
            dma((2,)),
            dma((2,)),
            dma((2,)),
            dma((2,)),
            pltpu.SemaphoreType.REGULAR((2,)),
        ],
        compiler_params=pltpu.CompilerParams(
            collective_id=0, has_side_effects=True, vmem_limit_bytes=40 * 1024 * 1024
        ),
    )(
        *(
            pltpu.with_memory_space_constraint(value, pltpu.HBM)
            for value in (out_grad, routes.T, route_weight.T, saved_act.reshape(2, 16, 64, 256), w_down[0])
        )
    )
    d_act, d_weight, d_route = pl.pallas_call(
        finish,
        out_shape=shapes,
        in_specs=[anywhere] * 3,
        out_specs=(hbm,) * 3,
        scratch_shapes=[dma((6,))],
        compiler_params=pltpu.CompilerParams(vmem_limit_bytes=2 * 1024 * 1024),
    )(*results)
    return (
        d_act.reshape(saved_act.shape),
        d_weight[None],
        d_route.T,
    )


def solution(mesh):
    placed = (
        P(("expert", "etp", "dp"), None),
        P(("expert", "etp", "dp"), None),
        P(("expert", "etp", "dp"), None),
        P(None, "dp", "expert", None, "etp"),
        P("expert", "etp", None),
    )
    return jax.shard_map(
        per_device,
        mesh=mesh,
        in_specs=placed,
        out_specs=(
            P(None, "dp", "expert", None, "etp"),
            P("expert", "etp", "dp"),
            P(("expert", "etp", "dp"), None),
        ),
        check_vma=False,
    )
```

```python
import jax
import jax.numpy as jnp
from jax import lax
from jax.experimental import pallas as pl
from jax.experimental.pallas import tpu as pltpu
from jax.sharding import PartitionSpec as P

MESH = pl.DeviceIdType.MESH
F32 = jnp.float32
BF16 = jnp.bfloat16
D = 3072
HALF = D // 2
FOLD = D // 4
STEP = HALF // 4
NEAR = ((0, 1, 15, 2), (14, 13, 3, 4), (12, 11, 5, 6), (10, 9, 7, 8))


def iota(shape, axis):
    return lax.broadcasted_iota(jnp.int32, shape, axis)


def kernel(
    tok_hbm, route_hbm, weight_hbm, act_hbm, w_hbm,
    dact, dw, droute,
    tok_ref, route_ref, weight_ref, act, w, wt, outgoing, fold, zbuf, rows, hid, cgate, cup, hidt, drel, grad, grad_in,
    last, last_in, psum, psum_in, colsum, colsum_in, late_in,
    local_sem, zsend, zrecv, gsend, grecv, psend, precv, csend, crecv, lsend, lrecv, xsend, xrecv, far_sem,
):
    e = lax.axis_index("expert")
    t = lax.axis_index("etp")
    p = lax.axis_index("dp")
    x, y, zh = t // 8, (t // 2) % 4, t % 2
    z = zh * 8 + e
    col = x * 4 + y

    def at(xx, yy, zz):
        return (zz % 8, xx * 8 + yy * 2 + zz // 8, p)

    def at_col(cc):
        return at(cc // 4, cc % 4, z)

    sibling = (e, t, 1 - p)
    xr, xl, yr, yl = (x + 1) % 4, (x + 3) % 4, (y + 1) % 4, (y + 3) % 4

    loads = []
    for k, (src, dst) in enumerate(
        ((route_hbm, route_ref), (weight_hbm, weight_ref), (tok_hbm, tok_ref), (act_hbm, act), (w_hbm, w))
    ):
        loads.append(pltpu.make_async_copy(src, dst, local_sem.at[k]))
        loads[k].start()
    load_act, load_w = loads[3:]

    barrier = pltpu.get_barrier_semaphore()
    near = [at(x, y, (z + k) % 16) for k in (1, 15, 2, 14)]
    near += [at((x + k) % 4, y, z) for k in (1, 3, 2)] + [at(x, (y + k) % 4, z) for k in (1, 3, 2)] + [sibling]
    for device in near:
        pl.semaphore_signal(barrier, inc=1, device_id=device, device_id_type=MESH)

    def tell(i):
        for k in (2 << i, 16 - (2 << i)):
            pl.semaphore_signal(far_sem.at[i], inc=1, device_id=at(x, y, (z + k) % 16), device_id_type=MESH)

    spread = (iota((8, 128), 1) % 8 == iota((8, 128), 0)).astype(BF16)
    for k in range(3):
        loads[k].wait()
    routes = jnp.dot(route_ref[...].astype(F32).astype(BF16), spread, preferred_element_type=F32)
    gates = jnp.dot(weight_ref[...], spread, preferred_element_type=F32)
    row, lane = iota((128, 128), 0), iota((128, 128), 1)
    row_e = (row // 16).astype(F32)
    first, second = routes[0:1] == row_e, routes[1:2] == row_e
    named = jnp.logical_or(first, second)
    earlier = jnp.logical_and(row // 8 == lane // 8, row < lane).astype(BF16)
    rank = jnp.dot(named.astype(F32).astype(BF16), earlier, preferred_element_type=F32)
    hit = jnp.logical_and(named, rank == (row % 4).astype(F32))
    hit = jnp.logical_and(hit, (row // 4) % 4 == lane // 8)
    pick = jnp.where(hit, jnp.where(first, gates[0:1], gates[1:2]), 0.0).astype(BF16)
    token = tok_ref[...].astype(F32)
    folded = jnp.concatenate(
        [
            jnp.concatenate([token[:, h * HALF + i * STEP : h * HALF + (i + 1) * STEP] for h in range(2)], axis=1)
            for i in range(4)
        ],
        axis=0,
    )
    slots = jnp.dot(pick[:, 0:32], folded.astype(BF16), preferred_element_type=F32)
    outgoing[...] = slots.astype(BF16).reshape(8, 16, FOLD)

    pl.semaphore_wait(barrier, len(near))

    sends = []

    def along(j):
        for k, near in enumerate(NEAR[j]):
            if near == 0:
                continue
            zz = (z + 16 - near) % 16
            copy = pltpu.make_async_remote_copy(
                src_ref=outgoing.at[zz % 8],
                dst_ref=fold.at[x, y, k] if j == 0 else zbuf.at[j, k],
                send_sem=zsend.at[j, k],
                recv_sem=zrecv.at[j],
                device_id=at(x, y, zz),
                device_id_type=MESH,
            )
            copy.start()
            sends.append(copy)

    along(0)
    tell(0)
    fold[x, y, 0] = outgoing[e]

    mrow, mcol = iota((64, 64), 0), iota((64, 64), 1)
    unfold = jnp.logical_and(mrow // 16 == (mcol // 4) % 4, (mrow // 4) % 4 == mcol // 16)
    unfold = jnp.logical_and(unfold, mrow % 4 == mcol % 4).astype(F32).astype(BF16)

    def unfolded(block, j, xx, yy):
        flat = jnp.dot(unfold, block.reshape(64, FOLD), preferred_element_type=F32).astype(BF16)
        for h in range(2):
            for i in range(4):
                cols = slice(h * HALF + i * STEP, h * HALF + (i + 1) * STEP)
                rows[j, xx, yy, :, cols] = flat[i * 16 : (i + 1) * 16, h * STEP : (h + 1) * STEP]

    def arrive(j):
        landed = fold.at[x, y, pl.ds(1, 3)] if j == 0 else zbuf.at[j]
        pltpu.make_async_copy(landed, landed, zrecv.at[j]).wait()

    def assemble(j):
        arrive(j)
        unfolded(zbuf[j], j, x, y)

    def assemble_near():
        @pl.loop(0, 16)
        def _(c):
            unfolded(fold[c // 4, c % 4], 0, c // 4, c % 4)

    whole = (pl.ds(0, HALF), pl.ds(HALF, HALF))
    part = (
        (pl.ds(0, FOLD), pl.ds(FOLD, FOLD)),
        (pl.ds(HALF, FOLD), pl.ds(HALF + FOLD, FOLD)),
    )

    def push(j, slot, ref, target):
        copy = pltpu.make_async_remote_copy(
            src_ref=ref,
            dst_ref=ref,
            send_sem=gsend.at[j, slot],
            recv_sem=grecv.at[j, slot],
            device_id=target,
            device_id_type=MESH,
        )
        copy.start()
        sends.append(copy)
        return copy

    right, left = (at(xr, y, z), at(x, yr, z)), (at(xl, y, z), at(x, yl, z))
    across = (at((x + 2) % 4, y, z), at(x, (y + 2) % 4, z))

    def line(unit, h, xx, yy):
        if unit < 2:
            return fold.at[xx, yy, pl.ds(unit, 1 + 2 * unit), :, pl.ds(h * STEP, STEP)]
        return rows.at[unit - 1, xx, yy, :, whole[h]]

    def piece(unit, h, at_line, i):
        if unit < 2:
            both = pl.ds(2 * i, 2)
            return line(unit, h, *((both, at_line) if h == 0 else (at_line, both)))
        both = pl.ds(0, 4)
        return rows.at[unit - 1, *((both, at_line) if h == 0 else (at_line, both)), :, part[h][i]]

    def one(unit):
        copies = []
        for d, target in enumerate((across, right, left)):
            for h in range(2):
                copies.append(push(unit, 9 * h + d, line(unit, h, x, y), target[h]))
        return copies

    def two(unit, got):
        for copy in got:
            copy.wait_recv()
        copies = []
        for i in range(2):
            for d in range(2):
                for h in range(2):
                    ref = piece(unit, h, (y, x)[h], d if i == 0 else 1 - d)
                    copies.append(push(unit, 9 * h + 3 + 2 * i + d, ref, (right, left)[d][1 - h]))
        return copies

    def onward(unit, got):
        copies = []
        for d in range(2):
            for h in range(2):
                got[2 * d + h].wait_recv()
                side = ((yl, xl), (yr, xr))[d][h]
                copies.append(push(unit, 9 * h + 7 + d, piece(unit, h, side, d), (right, left)[d][1 - h]))
        return copies + got[4:]

    frow, fcol = iota((64, 64), 0), iota((64, 64), 1)

    def chunked(place):
        near = jnp.zeros((64, 64), jnp.int32)
        for k, value in enumerate(sum(NEAR, ())):
            near = jnp.where(place // 4 == k, value, near)
        return 4 * ((z + near) % 16) + place % 4

    gather = (fcol == chunked(frow)).astype(F32).astype(BF16)
    scatter = (frow == chunked(fcol)).astype(F32).astype(BF16)

    def prepare(part):
        @pl.loop(part * 4, part * 4 + 4)
        def _(c):
            g = jnp.dot(gather, act[0, c], preferred_element_type=F32)
            u = jnp.dot(gather, act[1, c], preferred_element_type=F32)
            sig = 1.0 / (1.0 + jnp.exp(-g))
            gs = g * sig
            h = gs * u
            slope = u * sig * (1.0 + g * (1.0 - sig))
            at_rows = pl.ds(pl.multiple_of(c * 16, 16), 16)
            for j in range(4):
                mine = slice(j * 16, (j + 1) * 16)
                hid[j, at_rows, :] = h[mine]
                cup[j, at_rows, :] = gs[mine]
                cgate[j, at_rows, :] = slope[mine]

    def flip():
        for j in range(4):
            hidt[j] = hid[j].T.astype(BF16)

    def transpose_w():
        @pl.loop(0, D // 256)
        def _(k):
            at_cols = pl.ds(pl.multiple_of(k * 256, 256), 256)
            wt[at_cols, :] = w[:, at_cols].astype(F32).T.astype(BF16)

    def first_product(j):
        d_out = jnp.dot(rows[j].reshape(256, D), wt[...], preferred_element_type=F32)
        prod = d_out * hid[j]
        total = jnp.sum((prod[:, 0:128] + prod[:, 128:256]).T, axis=0, keepdims=True)
        psum[0, j, :, :] = total[:, 0:128]
        psum[1, j, :, :] = total[:, 128:256]
        return d_out

    def slopes(j, d_out):
        drel[0, :, j] = (d_out * cgate[j]).astype(BF16).reshape(16, 16, 256)
        drel[1, :, j] = (d_out * cup[j]).astype(BF16).reshape(16, 16, 256)

    def second_product(j, half, store):
        for k in range(3):
            in_cols = pl.ds(pl.multiple_of(half * HALF + k * 512, 512), 512)
            block = rows[j, :, :, :, in_cols].reshape(256, 512)
            store(slice(k * 512, (k + 1) * 512), jnp.dot(hidt[j], block, preferred_element_type=F32))

    def compute(j):
        slopes(j, first_product(j))
        for half in range(2):

            def store(cols, term):
                grad[half, :, cols] = term if j == 0 else grad[half, :, cols] + term

            second_product(j, half, store)

    early = pl.ds(0, 2)

    def to_columns():
        for k in range(1, 16):
            cc = (col + k) % 16
            copy = pltpu.make_async_remote_copy(
                src_ref=psum.at[cc // 8, early],
                dst_ref=psum_in.at[col],
                send_sem=psend.at[k - 1],
                recv_sem=precv,
                device_id=at_col(cc),
                device_id_type=MESH,
            )
            copy.start()
            sends.append(copy)
        psum_in[col] = psum[col // 8, early]

    def along_column():
        arrived = psum_in.at[pl.ds(0, 15)]
        pltpu.make_async_copy(arrived, arrived, precv).wait()
        for j in range(2):
            total = jnp.sum(psum_in[:, j], axis=0)
            for k, near in enumerate(NEAR[j]):
                turned = total if k == 0 else jnp.concatenate([total[:, 4 * k :], total[:, : 4 * k]], axis=1)
                colsum[j, k] = turned
                if near == 0:
                    colsum_in[z] = turned
                    continue
                copy = pltpu.make_async_remote_copy(
                    src_ref=colsum.at[j, k],
                    dst_ref=colsum_in.at[z],
                    send_sem=csend.at[j, k],
                    recv_sem=crecv,
                    device_id=at(x, y, (z + near) % 16),
                    device_id_type=MESH,
                )
                copy.start()
                sends.append(copy)

    def to_tokens(j):
        for i in (10, 11, 9, 14, 6, 15, 13, 7, 5, 8, 2, 12, 4, 3, 1, 0):
            cc = ((x + i // 4) % 4) * 4 + (y + i % 4) % 4
            for k, near in enumerate(NEAR[j]):
                copy = pltpu.make_async_remote_copy(
                    src_ref=psum.at[cc // 8, j],
                    dst_ref=late_in.at[j - 2, k, col],
                    send_sem=lsend.at[j - 2],
                    recv_sem=lrecv.at[j - 2],
                    device_id=(
                        (z + near) % 8,
                        (cc // 4) * 8 + (cc % 4) * 2 + ((z + near) % 16) // 8,
                        p,
                    ),
                    device_id_type=MESH,
                )
                copy.start()

    def landed(copies):
        for copy in copies:
            copy.wait_recv()

    am = one(0)
    pl.semaphore_wait(far_sem.at[0], 2)
    tell(1)
    along(1)
    bm = two(0, am)
    arrive(0)
    a0 = one(1)
    cm = onward(0, bm)
    pl.semaphore_wait(far_sem.at[1], 2)
    along(2)
    along(3)
    load_act.wait()
    prepare(0)
    b0 = two(1, a0)
    assemble(1)
    a1 = one(2)
    prepare(1)
    c0 = onward(1, b0)
    prepare(2)
    b1 = two(2, a1)
    prepare(3)
    load_w.wait()
    transpose_w()
    flip()
    assemble(2)
    a2 = one(3)
    c1 = onward(2, b1)
    landed(cm)
    landed(c0)
    assemble_near()
    compute(0)
    b2 = two(3, a2)
    assemble(3)
    a3 = one(4)
    c2 = onward(3, b2)
    landed(c1)
    compute(1)
    to_columns()
    b3 = two(4, a3)
    landed(c2)
    compute(2)
    c3 = onward(4, b3)
    to_tokens(2)
    along_column()

    def to_sibling(i, src, dst):
        copy = pltpu.make_async_remote_copy(
            src_ref=src, dst_ref=dst, send_sem=xsend.at[i], recv_sem=xrecv.at[i], device_id=sibling, device_id_type=MESH
        )
        copy.start()
        sends.append(copy)
        return copy

    under_way = len(sends) - 18 - 15 - 7
    for copy in sends[:under_way]:
        copy.wait_send()
    sends = sends[under_way:]
    most = to_sibling(0, grad.at[1 - p], grad_in)
    landed(c3)
    d_out = first_product(3)
    to_tokens(3)

    def store_last(cols, term):
        last[:, cols] = term.astype(BF16)

    def store_grad(cols, term):
        grad[p, :, cols] += term

    second_product(3, 1 - p, store_last)
    rest = to_sibling(1, last, last_in)
    slopes(3, d_out)
    second_product(3, p, store_grad)
    for i in range(2):
        for c in range(16):
            dact[i, c] = jnp.dot(scatter, drel[i, c].reshape(64, 256), preferred_element_type=F32).astype(BF16)

    most.wait_recv()
    rest.wait_recv()
    for k in range(3):
        cols = slice(k * 512, (k + 1) * 512)
        dw[:, cols] = (grad[p, :, cols] + grad_in[:, cols] + last_in[:, cols].astype(F32)).astype(BF16)
    arrived = colsum_in.at[pl.ds(0, 7)]
    pltpu.make_async_copy(arrived, arrived, crecv).wait()
    for j in (2, 3):
        late = late_in.at[j - 2]
        pltpu.make_async_copy(late, late, lrecv.at[j - 2]).wait()
        for k, near in enumerate(NEAR[j]):
            total = jnp.sum(late_in[j - 2, k], axis=0)
            turned = total if k == 0 else jnp.concatenate([total[:, 4 * k :], total[:, : 4 * k]], axis=1)
            colsum_in[(z + 16 - near) % 16] = turned
    value = jnp.zeros((128, 128), F32)
    for i in range(8):
        both = colsum_in[i] + colsum_in[i + 8]
        value = jnp.where(row // 16 == i, both, value)
    mine = (col % 8) * 16
    value = jnp.sum(jnp.where(lane == mine + row % 4, value, 0.0), axis=1, keepdims=True)
    for k, match in enumerate((first, second)):
        chosen = jnp.where(jnp.logical_and(hit, match), value, 0.0)
        score = jnp.sum(chosen, axis=0, keepdims=True) / gates[k : k + 1]
        droute[k : k + 1, :] = score[:, 0:8]
    for copy in sends:
        copy.wait_send()
    for i in range(2):
        pltpu.make_async_copy(late_in.at[i], late_in.at[i], lsend.at[i]).wait()


def finish(dact_in, dw_in, droute_in, dact, dw, droute, sem):
    copies = [pltpu.make_async_copy(dw_in, dw, sem.at[0]), pltpu.make_async_copy(droute_in, droute, sem.at[1])]
    for i in range(4):
        quarter = pl.ds(4 * i, 4)
        copies.append(pltpu.make_async_copy(dact_in.at[:, quarter], dact.at[:, quarter], sem.at[2 + i]))
    for copy in copies:
        copy.start()
    for copy in copies:
        copy.wait()


def per_device(out_grad, routes, route_weight, saved_act, w_down):
    hbm, anywhere = pl.BlockSpec(memory_space=pltpu.HBM), pl.BlockSpec(memory_space=pl.ANY)
    shapes = (
        jax.ShapeDtypeStruct((2, 16, 64, 256), BF16),
        jax.ShapeDtypeStruct((256, HALF), BF16),
        jax.ShapeDtypeStruct((2, 8), F32),
    )
    dma = pltpu.SemaphoreType.DMA
    results = pl.pallas_call(
        kernel,
        out_shape=shapes,
        in_specs=[hbm] * 5,
        out_specs=(pl.BlockSpec(memory_space=pltpu.VMEM),) * 3,
        scratch_shapes=[
            pltpu.VMEM((8, D), BF16),
            pltpu.VMEM((2, 8), jnp.int32),
            pltpu.VMEM((2, 8), BF16),
            pltpu.VMEM((2, 16, 64, 256), BF16),
            pltpu.VMEM((256, D), BF16),
            pltpu.VMEM((D, 256), BF16),
            pltpu.VMEM((8, 16, FOLD), BF16),
            pltpu.VMEM((4, 4, 4, 16, FOLD), BF16),
            pltpu.VMEM((4, 4, 16, FOLD), BF16),
            pltpu.VMEM((4, 4, 4, 16, D), BF16),
            pltpu.VMEM((4, 256, 256), F32),
            pltpu.VMEM((4, 256, 256), F32),
            pltpu.VMEM((4, 256, 256), F32),
            pltpu.VMEM((4, 256, 256), BF16),
            pltpu.VMEM((2, 16, 4, 16, 256), BF16),
            pltpu.VMEM((2, 256, HALF), F32),
            pltpu.VMEM((256, HALF), F32),
            pltpu.VMEM((256, HALF), BF16),
            pltpu.VMEM((256, HALF), BF16),
            pltpu.VMEM((2, 4, 1, 128), F32),
            pltpu.VMEM((16, 2, 1, 128), F32),
            pltpu.VMEM((2, 4, 1, 128), F32),
            pltpu.VMEM((16, 1, 128), F32),
            pltpu.VMEM((2, 4, 16, 1, 128), F32),
            dma((5,)),
            dma((4, 4)),
            dma((4,)),
            dma((5, 18)),
            dma((5, 18)),
            dma((15,)),
            dma,
            dma((2, 4)),
            dma,
            dma((2,)),
            dma((2,)),
            dma((2,)),
            dma((2,)),
            pltpu.SemaphoreType.REGULAR((2,)),
        ],
        compiler_params=pltpu.CompilerParams(
            collective_id=0, has_side_effects=True, vmem_limit_bytes=40 * 1024 * 1024
        ),
    )(
        *(
            pltpu.with_memory_space_constraint(value, pltpu.HBM)
            for value in (out_grad, routes.T, route_weight.T, saved_act.reshape(2, 16, 64, 256), w_down[0])
        )
    )
    d_act, d_weight, d_route = pl.pallas_call(
        finish,
        out_shape=shapes,
        in_specs=[anywhere] * 3,
        out_specs=(hbm,) * 3,
        scratch_shapes=[dma((6,))],
        compiler_params=pltpu.CompilerParams(vmem_limit_bytes=2 * 1024 * 1024),
    )(*results)
    return (
        d_act.reshape(saved_act.shape),
        d_weight[None],
        d_route.T,
    )


def solution(mesh):
    placed = (
        P(("expert", "etp", "dp"), None),
        P(("expert", "etp", "dp"), None),
        P(("expert", "etp", "dp"), None),
        P(None, "dp", "expert", None, "etp"),
        P("expert", "etp", None),
    )
    return jax.shard_map(
        per_device,
        mesh=mesh,
        in_specs=placed,
        out_specs=(
            P(None, "dp", "expert", None, "etp"),
            P("expert", "etp", "dp"),
            P(("expert", "etp", "dp"), None),
        ),
        check_vma=False,
    )
```

```python
import jax
import jax.numpy as jnp
from jax import lax
from jax.experimental import pallas as pl
from jax.experimental.pallas import tpu as pltpu
from jax.sharding import PartitionSpec as P

MESH = pl.DeviceIdType.MESH
F32 = jnp.float32
BF16 = jnp.bfloat16
D = 3072
HALF = D // 2
FOLD = D // 4
STEP = HALF // 4
NEAR = ((0, 1, 15, 2), (14, 13, 3, 4), (12, 11, 5, 6), (10, 9, 7, 8))


def iota(shape, axis):
    return lax.broadcasted_iota(jnp.int32, shape, axis)


def kernel(
    tok_hbm, route_hbm, weight_hbm, act_hbm, w_hbm,
    dact, dw, droute,
    tok_ref, route_ref, weight_ref, act, w, wt, outgoing, fold, zbuf, rows, hid, cgate, cup, hidt, drel, grad, grad_in,
    last, last_in, psum, psum_in, colsum, colsum_in, late_in,
    local_sem, zsend, zrecv, gsend, grecv, psend, precv, csend, crecv, lsend, lrecv, xsend, xrecv, far_sem,
):
    e = lax.axis_index("expert")
    t = lax.axis_index("etp")
    p = lax.axis_index("dp")
    x, y, zh = t // 8, (t // 2) % 4, t % 2
    z = zh * 8 + e
    col = x * 4 + y

    def at(xx, yy, zz):
        return (zz % 8, xx * 8 + yy * 2 + zz // 8, p)

    def at_col(cc):
        return at(cc // 4, cc % 4, z)

    sibling = (e, t, 1 - p)
    xr, xl, yr, yl = (x + 1) % 4, (x + 3) % 4, (y + 1) % 4, (y + 3) % 4

    loads = []
    for k, (src, dst) in enumerate(
        ((route_hbm, route_ref), (weight_hbm, weight_ref), (tok_hbm, tok_ref), (act_hbm, act), (w_hbm, w))
    ):
        loads.append(pltpu.make_async_copy(src, dst, local_sem.at[k]))
        loads[k].start()
    load_act, load_w = loads[3:]

    barrier = pltpu.get_barrier_semaphore()
    near = [at(x, y, (z + k) % 16) for k in (1, 15, 2, 14)]
    near += [at((x + k) % 4, y, z) for k in (1, 3, 2)] + [at(x, (y + k) % 4, z) for k in (1, 3, 2)] + [sibling]
    for device in near:
        pl.semaphore_signal(barrier, inc=1, device_id=device, device_id_type=MESH)

    def tell(i):
        for k in (2 << i, 16 - (2 << i)):
            pl.semaphore_signal(far_sem.at[i], inc=1, device_id=at(x, y, (z + k) % 16), device_id_type=MESH)

    spread = (iota((8, 128), 1) % 8 == iota((8, 128), 0)).astype(BF16)
    for k in range(3):
        loads[k].wait()
    routes = jnp.dot(route_ref[...].astype(F32).astype(BF16), spread, preferred_element_type=F32)
    gates = jnp.dot(weight_ref[...], spread, preferred_element_type=F32)
    row, lane = iota((128, 128), 0), iota((128, 128), 1)
    row_e = (row // 16).astype(F32)
    first, second = routes[0:1] == row_e, routes[1:2] == row_e
    named = jnp.logical_or(first, second)
    earlier = jnp.logical_and(row // 8 == lane // 8, row < lane).astype(BF16)
    rank = jnp.dot(named.astype(F32).astype(BF16), earlier, preferred_element_type=F32)
    hit = jnp.logical_and(named, rank == (row % 4).astype(F32))
    hit = jnp.logical_and(hit, (row // 4) % 4 == lane // 8)
    pick = jnp.where(hit, jnp.where(first, gates[0:1], gates[1:2]), 0.0).astype(BF16)
    token = tok_ref[...].astype(F32)
    folded = jnp.concatenate(
        [
            jnp.concatenate([token[:, h * HALF + i * STEP : h * HALF + (i + 1) * STEP] for h in range(2)], axis=1)
            for i in range(4)
        ],
        axis=0,
    )
    slots = jnp.dot(pick[:, 0:32], folded.astype(BF16), preferred_element_type=F32)
    outgoing[...] = slots.astype(BF16).reshape(8, 16, FOLD)

    pl.semaphore_wait(barrier, len(near))

    sends = []

    def along(j):
        for k, near in enumerate(NEAR[j]):
            if near == 0:
                continue
            zz = (z + 16 - near) % 16
            copy = pltpu.make_async_remote_copy(
                src_ref=outgoing.at[zz % 8],
                dst_ref=fold.at[x, y, k] if j == 0 else zbuf.at[j, k],
                send_sem=zsend.at[j, k],
                recv_sem=zrecv.at[j],
                device_id=at(x, y, zz),
                device_id_type=MESH,
            )
            copy.start()
            sends.append(copy)

    along(0)
    tell(0)
    fold[x, y, 0] = outgoing[e]

    mrow, mcol = iota((64, 64), 0), iota((64, 64), 1)
    unfold = jnp.logical_and(mrow // 16 == (mcol // 4) % 4, (mrow // 4) % 4 == mcol // 16)
    unfold = jnp.logical_and(unfold, mrow % 4 == mcol % 4).astype(F32).astype(BF16)

    def unfolded(block, j, xx, yy):
        flat = jnp.dot(unfold, block.reshape(64, FOLD), preferred_element_type=F32).astype(BF16)
        for h in range(2):
            for i in range(4):
                cols = slice(h * HALF + i * STEP, h * HALF + (i + 1) * STEP)
                rows[j, xx, yy, :, cols] = flat[i * 16 : (i + 1) * 16, h * STEP : (h + 1) * STEP]

    def arrive(j):
        landed = fold.at[x, y, pl.ds(1, 3)] if j == 0 else zbuf.at[j]
        pltpu.make_async_copy(landed, landed, zrecv.at[j]).wait()

    def assemble(j):
        arrive(j)
        unfolded(zbuf[j], j, x, y)

    def assemble_near():
        @pl.loop(0, 16)
        def _(c):
            unfolded(fold[c // 4, c % 4], 0, c // 4, c % 4)

    whole = (pl.ds(0, HALF), pl.ds(HALF, HALF))
    part = (
        (pl.ds(0, FOLD), pl.ds(FOLD, FOLD)),
        (pl.ds(HALF, FOLD), pl.ds(HALF + FOLD, FOLD)),
    )

    def push(j, slot, ref, target):
        copy = pltpu.make_async_remote_copy(
            src_ref=ref,
            dst_ref=ref,
            send_sem=gsend.at[j, slot],
            recv_sem=grecv.at[j, slot],
            device_id=target,
            device_id_type=MESH,
        )
        copy.start()
        sends.append(copy)
        return copy

    right, left = (at(xr, y, z), at(x, yr, z)), (at(xl, y, z), at(x, yl, z))
    across = (at((x + 2) % 4, y, z), at(x, (y + 2) % 4, z))

    def line(unit, h, xx, yy):
        if unit < 2:
            return fold.at[xx, yy, pl.ds(unit, 1 + 2 * unit), :, pl.ds(h * STEP, STEP)]
        return rows.at[unit - 1, xx, yy, :, whole[h]]

    def piece(unit, h, at_line, i):
        if unit < 2:
            both = pl.ds(2 * i, 2)
            return line(unit, h, *((both, at_line) if h == 0 else (at_line, both)))
        both = pl.ds(0, 4)
        return rows.at[unit - 1, *((both, at_line) if h == 0 else (at_line, both)), :, part[h][i]]

    def one(unit):
        copies = []
        for d, target in enumerate((across, right, left)):
            for h in range(2):
                copies.append(push(unit, 9 * h + d, line(unit, h, x, y), target[h]))
        return copies

    def two(unit, got):
        for copy in got:
            copy.wait_recv()
        copies = []
        for i in range(2):
            for d in range(2):
                for h in range(2):
                    ref = piece(unit, h, (y, x)[h], d if i == 0 else 1 - d)
                    copies.append(push(unit, 9 * h + 3 + 2 * i + d, ref, (right, left)[d][1 - h]))
        return copies

    def onward(unit, got):
        copies = []
        for d in range(2):
            for h in range(2):
                got[2 * d + h].wait_recv()
                side = ((yl, xl), (yr, xr))[d][h]
                copies.append(push(unit, 9 * h + 7 + d, piece(unit, h, side, d), (right, left)[d][1 - h]))
        return copies + got[4:]

    frow, fcol = iota((64, 64), 0), iota((64, 64), 1)

    def chunked(place):
        near = jnp.zeros((64, 64), jnp.int32)
        for k, value in enumerate(sum(NEAR, ())):
            near = jnp.where(place // 4 == k, value, near)
        return 4 * ((z + near) % 16) + place % 4

    gather = (fcol == chunked(frow)).astype(F32).astype(BF16)
    scatter = (frow == chunked(fcol)).astype(F32).astype(BF16)

    def prepare(part):
        @pl.loop(part * 4, part * 4 + 4)
        def _(c):
            g = jnp.dot(gather, act[0, c], preferred_element_type=F32)
            u = jnp.dot(gather, act[1, c], preferred_element_type=F32)
            sig = 1.0 / (1.0 + jnp.exp(-g))
            gs = g * sig
            h = gs * u
            slope = u * sig * (1.0 + g * (1.0 - sig))
            at_rows = pl.ds(pl.multiple_of(c * 16, 16), 16)
            for j in range(4):
                mine = slice(j * 16, (j + 1) * 16)
                hid[j, at_rows, :] = h[mine]
                cup[j, at_rows, :] = gs[mine]
                cgate[j, at_rows, :] = slope[mine]

    def flip():
        for j in range(4):
            hidt[j] = hid[j].T.astype(BF16)

    def transpose_w():
        @pl.loop(0, D // 256)
        def _(k):
            at_cols = pl.ds(pl.multiple_of(k * 256, 256), 256)
            wt[at_cols, :] = w[:, at_cols].astype(F32).T.astype(BF16)

    def first_product(j):
        d_out = jnp.dot(rows[j].reshape(256, D), wt[...], preferred_element_type=F32)
        prod = d_out * hid[j]
        total = jnp.sum((prod[:, 0:128] + prod[:, 128:256]).T, axis=0, keepdims=True)
        psum[0, j, :, :] = total[:, 0:128]
        psum[1, j, :, :] = total[:, 128:256]
        return d_out

    def slopes(j, d_out):
        drel[0, :, j] = (d_out * cgate[j]).astype(BF16).reshape(16, 16, 256)
        drel[1, :, j] = (d_out * cup[j]).astype(BF16).reshape(16, 16, 256)

    def second_product(j, half, store):
        for k in range(3):
            in_cols = pl.ds(pl.multiple_of(half * HALF + k * 512, 512), 512)
            block = rows[j, :, :, :, in_cols].reshape(256, 512)
            store(slice(k * 512, (k + 1) * 512), jnp.dot(hidt[j], block, preferred_element_type=F32))

    def compute(j):
        slopes(j, first_product(j))
        for half in range(2):

            def store(cols, term):
                grad[half, :, cols] = term if j == 0 else grad[half, :, cols] + term

            second_product(j, half, store)

    early = pl.ds(0, 2)

    def to_columns():
        for k in range(1, 16):
            cc = (col + k) % 16
            copy = pltpu.make_async_remote_copy(
                src_ref=psum.at[cc // 8, early],
                dst_ref=psum_in.at[col],
                send_sem=psend.at[k - 1],
                recv_sem=precv,
                device_id=at_col(cc),
                device_id_type=MESH,
            )
            copy.start()
            sends.append(copy)
        psum_in[col] = psum[col // 8, early]

    def along_column():
        arrived = psum_in.at[pl.ds(0, 15)]
        pltpu.make_async_copy(arrived, arrived, precv).wait()
        for j in range(2):
            total = jnp.sum(psum_in[:, j], axis=0)
            for k, near in enumerate(NEAR[j]):
                turned = total if k == 0 else jnp.concatenate([total[:, 4 * k :], total[:, : 4 * k]], axis=1)
                colsum[j, k] = turned
                if near == 0:
                    colsum_in[z] = turned
                    continue
                copy = pltpu.make_async_remote_copy(
                    src_ref=colsum.at[j, k],
                    dst_ref=colsum_in.at[z],
                    send_sem=csend.at[j, k],
                    recv_sem=crecv,
                    device_id=at(x, y, (z + near) % 16),
                    device_id_type=MESH,
                )
                copy.start()
                sends.append(copy)

    def to_tokens(j):
        for i in (10, 11, 9, 14, 6, 15, 13, 7, 5, 8, 2, 12, 4, 3, 1, 0):
            cc = ((x + i // 4) % 4) * 4 + (y + i % 4) % 4
            for k, near in enumerate(NEAR[j]):
                copy = pltpu.make_async_remote_copy(
                    src_ref=psum.at[cc // 8, j],
                    dst_ref=late_in.at[j - 2, k, col],
                    send_sem=lsend.at[j - 2],
                    recv_sem=lrecv.at[j - 2],
                    device_id=(
                        (z + near) % 8,
                        (cc // 4) * 8 + (cc % 4) * 2 + ((z + near) % 16) // 8,
                        p,
                    ),
                    device_id_type=MESH,
                )
                copy.start()

    def landed(copies):
        for copy in copies:
            copy.wait_recv()

    am = one(0)
    pl.semaphore_wait(far_sem.at[0], 2)
    tell(1)
    along(1)
    bm = two(0, am)
    arrive(0)
    a0 = one(1)
    cm = onward(0, bm)
    pl.semaphore_wait(far_sem.at[1], 2)
    along(2)
    along(3)
    load_act.wait()
    prepare(0)
    b0 = two(1, a0)
    assemble(1)
    a1 = one(2)
    prepare(1)
    c0 = onward(1, b0)
    prepare(2)
    b1 = two(2, a1)
    prepare(3)
    assemble(2)
    a2 = one(3)
    c1 = onward(2, b1)
    load_w.wait()
    transpose_w()
    flip()
    b2 = two(3, a2)
    assemble(3)
    a3 = one(4)
    landed(cm)
    landed(c0)
    assemble_near()
    compute(0)
    c2 = onward(3, b2)
    b3 = two(4, a3)
    landed(c1)
    compute(1)
    to_columns()
    landed(c2)
    compute(2)
    c3 = onward(4, b3)
    to_tokens(2)
    along_column()

    def to_sibling(i, src, dst):
        copy = pltpu.make_async_remote_copy(
            src_ref=src, dst_ref=dst, send_sem=xsend.at[i], recv_sem=xrecv.at[i], device_id=sibling, device_id_type=MESH
        )
        copy.start()
        sends.append(copy)
        return copy

    under_way = len(sends) - 18 - 15 - 7
    for copy in sends[:under_way]:
        copy.wait_send()
    sends = sends[under_way:]
    most = to_sibling(0, grad.at[1 - p], grad_in)
    landed(c3)
    d_out = first_product(3)
    to_tokens(3)

    def store_last(cols, term):
        last[:, cols] = term.astype(BF16)

    def store_grad(cols, term):
        grad[p, :, cols] += term

    second_product(3, 1 - p, store_last)
    rest = to_sibling(1, last, last_in)
    slopes(3, d_out)
    second_product(3, p, store_grad)
    for i in range(2):
        for c in range(16):
            dact[i, c] = jnp.dot(scatter, drel[i, c].reshape(64, 256), preferred_element_type=F32).astype(BF16)

    most.wait_recv()
    rest.wait_recv()
    for k in range(3):
        cols = slice(k * 512, (k + 1) * 512)
        dw[:, cols] = (grad[p, :, cols] + grad_in[:, cols] + last_in[:, cols].astype(F32)).astype(BF16)
    arrived = colsum_in.at[pl.ds(0, 7)]
    pltpu.make_async_copy(arrived, arrived, crecv).wait()
    for j in (2, 3):
        late = late_in.at[j - 2]
        pltpu.make_async_copy(late, late, lrecv.at[j - 2]).wait()
        for k, near in enumerate(NEAR[j]):
            total = jnp.sum(late_in[j - 2, k], axis=0)
            turned = total if k == 0 else jnp.concatenate([total[:, 4 * k :], total[:, : 4 * k]], axis=1)
            colsum_in[(z + 16 - near) % 16] = turned
    value = jnp.zeros((128, 128), F32)
    for i in range(8):
        both = colsum_in[i] + colsum_in[i + 8]
        value = jnp.where(row // 16 == i, both, value)
    mine = (col % 8) * 16
    value = jnp.sum(jnp.where(lane == mine + row % 4, value, 0.0), axis=1, keepdims=True)
    for k, match in enumerate((first, second)):
        chosen = jnp.where(jnp.logical_and(hit, match), value, 0.0)
        score = jnp.sum(chosen, axis=0, keepdims=True) / gates[k : k + 1]
        droute[k : k + 1, :] = score[:, 0:8]
    for copy in sends:
        copy.wait_send()
    for i in range(2):
        pltpu.make_async_copy(late_in.at[i], late_in.at[i], lsend.at[i]).wait()


def finish(dact_in, dw_in, droute_in, dact, dw, droute, sem):
    copies = [pltpu.make_async_copy(dw_in, dw, sem.at[0]), pltpu.make_async_copy(droute_in, droute, sem.at[1])]
    for i in range(4):
        quarter = pl.ds(4 * i, 4)
        copies.append(pltpu.make_async_copy(dact_in.at[:, quarter], dact.at[:, quarter], sem.at[2 + i]))
    for copy in copies:
        copy.start()
    for copy in copies:
        copy.wait()


def per_device(out_grad, routes, route_weight, saved_act, w_down):
    hbm, anywhere = pl.BlockSpec(memory_space=pltpu.HBM), pl.BlockSpec(memory_space=pl.ANY)
    shapes = (
        jax.ShapeDtypeStruct((2, 16, 64, 256), BF16),
        jax.ShapeDtypeStruct((256, HALF), BF16),
        jax.ShapeDtypeStruct((2, 8), F32),
    )
    dma = pltpu.SemaphoreType.DMA
    results = pl.pallas_call(
        kernel,
        out_shape=shapes,
        in_specs=[hbm] * 5,
        out_specs=(pl.BlockSpec(memory_space=pltpu.VMEM),) * 3,
        scratch_shapes=[
            pltpu.VMEM((8, D), BF16),
            pltpu.VMEM((2, 8), jnp.int32),
            pltpu.VMEM((2, 8), BF16),
            pltpu.VMEM((2, 16, 64, 256), BF16),
            pltpu.VMEM((256, D), BF16),
            pltpu.VMEM((D, 256), BF16),
            pltpu.VMEM((8, 16, FOLD), BF16),
            pltpu.VMEM((4, 4, 4, 16, FOLD), BF16),
            pltpu.VMEM((4, 4, 16, FOLD), BF16),
            pltpu.VMEM((4, 4, 4, 16, D), BF16),
            pltpu.VMEM((4, 256, 256), F32),
            pltpu.VMEM((4, 256, 256), F32),
            pltpu.VMEM((4, 256, 256), F32),
            pltpu.VMEM((4, 256, 256), BF16),
            pltpu.VMEM((2, 16, 4, 16, 256), BF16),
            pltpu.VMEM((2, 256, HALF), F32),
            pltpu.VMEM((256, HALF), F32),
            pltpu.VMEM((256, HALF), BF16),
            pltpu.VMEM((256, HALF), BF16),
            pltpu.VMEM((2, 4, 1, 128), F32),
            pltpu.VMEM((16, 2, 1, 128), F32),
            pltpu.VMEM((2, 4, 1, 128), F32),
            pltpu.VMEM((16, 1, 128), F32),
            pltpu.VMEM((2, 4, 16, 1, 128), F32),
            dma((5,)),
            dma((4, 4)),
            dma((4,)),
            dma((5, 18)),
            dma((5, 18)),
            dma((15,)),
            dma,
            dma((2, 4)),
            dma,
            dma((2,)),
            dma((2,)),
            dma((2,)),
            dma((2,)),
            pltpu.SemaphoreType.REGULAR((2,)),
        ],
        compiler_params=pltpu.CompilerParams(
            collective_id=0, has_side_effects=True, vmem_limit_bytes=40 * 1024 * 1024
        ),
    )(
        *(
            pltpu.with_memory_space_constraint(value, pltpu.HBM)
            for value in (out_grad, routes.T, route_weight.T, saved_act.reshape(2, 16, 64, 256), w_down[0])
        )
    )
    d_act, d_weight, d_route = pl.pallas_call(
        finish,
        out_shape=shapes,
        in_specs=[anywhere] * 3,
        out_specs=(hbm,) * 3,
        scratch_shapes=[dma((6,))],
        compiler_params=pltpu.CompilerParams(vmem_limit_bytes=2 * 1024 * 1024),
    )(*results)
    return (
        d_act.reshape(saved_act.shape),
        d_weight[None],
        d_route.T,
    )


def solution(mesh):
    placed = (
        P(("expert", "etp", "dp"), None),
        P(("expert", "etp", "dp"), None),
        P(("expert", "etp", "dp"), None),
        P(None, "dp", "expert", None, "etp"),
        P("expert", "etp", None),
    )
    return jax.shard_map(
        per_device,
        mesh=mesh,
        in_specs=placed,
        out_specs=(
            P(None, "dp", "expert", None, "etp"),
            P("expert", "etp", "dp"),
            P(("expert", "etp", "dp"), None),
        ),
        check_vma=False,
    )
```
